32 devices in a mesh: groups: 2 (over y), pair: 8 (over z, x), virt: 2 (over core).
Axes of the slice: x: 2, y: 2, z: 4, core: 2. Of those that a mesh axis runs over, the one named last changes fastest.
Arguments:
- amp_tiles: bfloat16 [16, 16, 128, 128], P(('groups', 'pair'), 'virt'), parts along dimension 0, may hold values from -6 to 6
- tile_coords: int32 [16, 16, 2], P(('groups', 'pair')), parts along dimension 0, may hold values from 0 to 11, as said below
- tile_mask: int32 [16, 16], P(('groups', 'pair')), parts along dimension 0, may hold values 0 or 1
- pair_orbs: int32 [16, 2], P(('groups', 'pair')), parts along dimension 0, may hold values from 0 to 7, as said below
- ladder_factor: bfloat16 [4, 1536, 1536], P(('groups', 'virt')), parts along dimension 0, may hold values from -0.25 to 0.25
- cycle_factor: bfloat16 [16, 1536, 128], P('groups'), parts along dimension 0, may hold values from -0.1875 to 0.1875
Outputs:
- residual: bfloat16 [16, 1536, 1536], P(('groups', 'pair'), 'virt'), parts along dimension 0
The draws below stay inside these ranges and needn't reach their ends.
There are 2 independent parts, one for each index of `groups`. The reference program is written for one: setup_inputs(seed, part) draws one part's arguments, and reference() takes and returns one part's arrays. A program takes and returns all parts, laid end to end along the dimension named above; each array names one. Nothing has to cross between parts.
Inputs may be any that keep to these rules, and one draw needn't show every extreme that they name: `tile_coords`: row k of a pair holds the c tile and the d tile of slot k; the 16 slots of one pair name different tile pairs. `pair_orbs`: column 0 is i, column 1 is j; no two pairs are equal; pair p and pair p + 4 have the same j.
All inputs are finite; a program needn't handle non-finite values. No bound on the sum of `tile_mask` on one device may be relied on, other than what follows from the above.
Results may differ from the reference program's by a relative error of at most 0.0051.
Values may be sent and summed in bfloat16 or wider, within the bound.
No kernel may reach another device: no remote copies, remote signals or barrier semaphores. Data moves between devices by JAX's collectives and lax.ppermute only.
A program may use at most 128 MiB of HBM per device.

```python
import jax
import jax.numpy as jnp
from jax import lax

V = 1536
TILE = 128
NT = 12
NQ = 128
NQL = 2
O = 8
KT = 16
PAIRS = 8


def draw_tile_coords(key, part):
    key = jax.random.fold_in(key, 11)
    pair_keys = jax.random.split(key, PAIRS)
    chosen = jax.vmap(lambda single: jax.random.permutation(single, NT * NT)[:KT])(pair_keys)
    return jnp.stack([chosen // NT, chosen % NT], axis=-1).astype(jnp.int32)


def draw_pair_orbs(key, part):
    key = jax.random.fold_in(key, 23)
    chosen = jax.random.permutation(key, O // 2 * O)[:PAIRS // 2]
    first_i = chosen // O
    first_j = chosen % O
    left_half = jnp.stack([first_i, first_j], axis=-1)
    right_half = jnp.stack([first_i + O // 2, first_j], axis=-1)
    return jnp.concatenate([left_half, right_half], axis=0).astype(jnp.int32)


def touch_ends(array, own_key, smallest, top_value):
    longest = array.shape.index(max(array.shape))
    spots = []
    for shift in (0, 1):
        where = [jax.random.randint(jax.random.fold_in(own_key, axis), (), 0, length) for axis, length in enumerate(array.shape)]
        where[longest] = (where[longest] + shift) % array.shape[longest]
        spots.append(tuple(where))
    return array.at[spots[0]].set(smallest).at[spots[1]].set(top_value)


def block_levels(own_key, shape, shards, least, top_value):
    gain = 1.0
    for dim, blocks in shards:
        heights = jax.random.uniform(jax.random.fold_in(jax.random.fold_in(own_key, 6), dim), (blocks,), jnp.float32, least / len(shards), top_value / len(shards))
        gain = gain * jnp.repeat(jnp.exp(heights), shape[dim] // blocks).reshape((-1,) + (1,) * (len(shape) - 1 - dim))
    return gain


def centred(stream_key, extent, scale, limit, pieces=(), held_as=jnp.bfloat16):
    entries = scale * jax.random.normal(stream_key, extent, jnp.float32)
    if pieces:
        entries = entries * block_levels(stream_key, extent, pieces, -0.22, 0.18)
    return jnp.clip(entries, -limit, limit).astype(held_as)


def setup_inputs(seed: int = 0, part: int = 0) -> dict:
    arg_keys = jax.random.split(jax.random.key(seed), 7)
    part_keys = jax.random.split(jax.random.fold_in(arg_keys[6], part), 7)
    amp_tiles = centred(part_keys[0], (PAIRS, KT, TILE, TILE), 1.0, 6.0, ((0, 8), (1, 2)))
    tile_coords = draw_tile_coords(jax.random.fold_in(jax.random.fold_in(arg_keys[6], part), 71), part)
    tile_mask = touch_ends((jax.random.randint(part_keys[2], (PAIRS, KT), 0, 4) < 3).astype(jnp.int32), jax.random.fold_in(part_keys[2], 1), 0, 1)
    pair_orbs = draw_pair_orbs(jax.random.fold_in(jax.random.fold_in(arg_keys[6], part), 71), part)
    ladder_factor = centred(part_keys[4], (NQL, V, V), (TILE * 4) ** -0.5, 0.25, ((0, 2),))
    cycle_factor = centred(part_keys[5], (O, V, NQ), (TILE * 8) ** -0.5, 0.1875)
    return {"amp_tiles": amp_tiles, "tile_coords": tile_coords, "tile_mask": tile_mask, "pair_orbs": pair_orbs, "ladder_factor": ladder_factor, "cycle_factor": cycle_factor}


def reference(amp_tiles, tile_coords, tile_mask, pair_orbs, ladder_factor, cycle_factor):
    masked = amp_tiles.astype(jnp.float32) * tile_mask.astype(jnp.float32)[:, :, None, None]
    cycle_blocks = cycle_factor.astype(jnp.float32)

    def accumulate(totals, orbital_pair_entries):
        selected_tiles, coords, orbitals = orbital_pair_entries
        cycle_cols = cycle_blocks[orbitals[0]].reshape(NT, TILE, NQ)[coords[:, 0]]
        intermediate_terms = jnp.einsum('kcq,kcd->kqd', cycle_cols, selected_tiles)
        placed = (coords[:, 1][:, None] == jnp.arange(NT, dtype=jnp.int32)[None, :]).astype(jnp.float32)
        distribute_tiles = jnp.einsum('kn,kqd->qnd', placed, intermediate_terms).reshape(NQ, V)
        chosen = (jnp.arange(O, dtype=jnp.int32) == orbitals[1]).astype(jnp.float32)
        return totals + chosen[:, None, None] * distribute_tiles[None], None

    cycle_sums, _ = lax.scan(accumulate, jnp.zeros((O, NQ, V), jnp.float32), (masked, tile_coords, pair_orbs))
    cycle_low = cycle_sums.astype(jnp.bfloat16)

    def pair_residual(orbital_pair_entries):
        selected_tiles, coords, orbitals = orbital_pair_entries
        ladder = jnp.zeros((V, V), jnp.float32)
        for aux in range(NQL):
            factor_now = ladder_factor[aux]
            blocks = factor_now.astype(jnp.float32).reshape(V, NT, TILE)
            trailing_columns = blocks[:, coords[:, 1], :]
            contraction_block = jnp.einsum('ozg,tog->ozt', selected_tiles, trailing_columns).astype(jnp.bfloat16)
            left_cols = factor_now.reshape(V, NT, TILE)[:, coords[:, 0], :].reshape(V, KT * TILE)
            ladder = ladder + jnp.dot(left_cols, contraction_block.reshape(KT * TILE, V), preferred_element_type=jnp.float32)
        cycle_term = jnp.dot(cycle_factor[orbitals[0]], cycle_low[orbitals[1]], preferred_element_type=jnp.float32)
        return (ladder + cycle_term).astype(jnp.bfloat16)

    return lax.map(pair_residual, (masked, tile_coords, pair_orbs))
```

```python
import functools

import jax
import jax.numpy as jnp
from jax import lax
from jax.experimental import pallas as pl
from jax.experimental.pallas import tpu as pltpu
from jax.sharding import PartitionSpec as P

LANES = 128
SMEM = pl.BlockSpec(memory_space=pltpu.SMEM)
VMEM = pl.BlockSpec(memory_space=pltpu.VMEM)
ANY = pl.BlockSpec(memory_space=pl.ANY)
FIRST_FIRST = (((0,), (0,)), ((), ()))
LAST_LAST = (((1,), (1,)), ((), ()))


def params(mib):
    return pltpu.CompilerParams(vmem_limit_bytes=mib * 2**20)


def block(index, size):
    return pl.ds(pl.multiple_of(index * size, size), size)


def intermediate(coords, mask, orbs, place, own, other, cycle_factor, *, cores):
    slots = coords.shape[0]
    local, tile = own.shape[0], own.shape[1]
    width, aux = cycle_factor.shape[1:]
    share = aux // cores
    part = share // 2

    def body(coords, mask, orbs, place, own, other, factor, first, second, rows, total, sem):
        load = pltpu.make_async_copy(factor.at[orbs[0]], rows, sem)
        load.start()
        core = place[0]
        total[...] = jnp.zeros_like(total)
        load.wait()
        terms = []
        for s in range(slots):
            g = lax.rem(s + core * local, slots)
            held = own[s] if s < local else other[s - local]
            term = lax.dot_general(
                rows[block(coords[g, 0], tile), :], held, FIRST_FIRST,
                preferred_element_type=jnp.float32,
            )
            terms.append((g, term))
        for g, term in terms:
            total[:, block(coords[g, 1], tile)] += term * mask[g].astype(jnp.float32)
        first[...] = total[block(2 * core, part), :].astype(first.dtype)
        second[:, :width] = total[block(2 * core + 1, part), :].astype(second.dtype)
        label = jnp.zeros((part, LANES), jnp.float32) + orbs[1].astype(jnp.float32)
        second[:, width:] = label.astype(second.dtype)

    return pl.pallas_call(
        body,
        out_shape=[
            jax.ShapeDtypeStruct((part, width), jnp.bfloat16),
            jax.ShapeDtypeStruct((part, width + LANES), jnp.bfloat16),
        ],
        in_specs=[SMEM, SMEM, SMEM, SMEM, VMEM, VMEM, ANY],
        out_specs=[VMEM, VMEM],
        scratch_shapes=[
            pltpu.VMEM((width, aux), jnp.bfloat16),
            pltpu.VMEM((aux, width), jnp.float32),
            pltpu.SemaphoreType.DMA,
        ],
        compiler_params=params(16),
        name="intermediate",
    )(coords, mask, orbs, place, own, other, cycle_factor)


def same_orbital(mine, theirs, width):
    return (mine[:, width : width + 1] == theirs[:, width : width + 1]).astype(jnp.float32)


def sum_middle(first, first_far, second, second_near):
    width = first.shape[1]

    def body(first, first_far, second, *refs):
        near, (first_out, second_out) = refs[:-2], refs[-2:]
        first_out[...] = (first[...].astype(jnp.float32) + first_far[...].astype(jnp.float32)).astype(jnp.bfloat16)
        total = second[:, :width].astype(jnp.float32)
        for theirs in near:
            weight = same_orbital(second[...].astype(jnp.float32), theirs[...].astype(jnp.float32), width)
            total += weight * theirs[:, :width].astype(jnp.float32)
        second_out[...] = total.astype(jnp.bfloat16)

    return pl.pallas_call(
        body,
        out_shape=[jax.ShapeDtypeStruct(first.shape, jnp.bfloat16)] * 2,
        in_specs=[VMEM] * (3 + len(second_near)),
        out_specs=[VMEM, VMEM],
        compiler_params=params(16),
        name="sum_middle",
    )(first, first_far, second, *second_near)


def sum_last(second, second_near, first_sum, first_sum_near, second_sum, second_sum_far):
    part, width = first_sum.shape
    count = len(second_near)

    def body(*refs):
        second, near = refs[0], refs[1 : 1 + count]
        first, first_near = refs[1 + count], refs[2 + count : 2 + 2 * count]
        second_sum, second_far, out = refs[2 + 2 * count :]
        total = first[...].astype(jnp.float32)
        for theirs, value in zip(near, first_near):
            weight = same_orbital(second[...].astype(jnp.float32), theirs[...].astype(jnp.float32), width)
            total += weight * value[...].astype(jnp.float32)
        out[:part, :] = total.astype(jnp.bfloat16)
        out[part:, :] = (second_sum[...].astype(jnp.float32) + second_far[...].astype(jnp.float32)).astype(jnp.bfloat16)

    return pl.pallas_call(
        body,
        out_shape=jax.ShapeDtypeStruct((2 * part, width), jnp.bfloat16),
        in_specs=[VMEM] * (4 + 2 * count),
        out_specs=VMEM,
        compiler_params=params(16),
        name="sum_last",
    )(second, *second_near, first_sum, *first_sum_near, second_sum, second_sum_far)


def ladder(coords, mask, place, own, other, factor, *, far, out_dtype):
    slots = coords.shape[0]
    local, tile = own.shape[0], own.shape[1]
    width = factor.shape[0]
    half = width // 2
    tiles = width // tile
    span = 2 * tile

    def body(coords, mask, place, own, other, factor, out, left, wide, held, head, link, names, starts):
        core = place[0]
        rows = block(1 - core if far else core, half)
        held[:local] = own[...]
        held[local:] = other[...]

        def clear(n, carry):
            head[n] = -1
            return carry

        lax.fori_loop(0, tiles, clear, 0)

        def put(s, carry):
            g = lax.rem(s + core * local, slots)
            d = coords[g, 1]

            @pl.when(mask[g] != 0)
            def _():
                link[s] = head[d]
                head[d] = s

            return carry

        lax.fori_loop(0, slots, put, 0)

        def name(n, count):
            names[count] = n
            starts[count] = head[n]
            return count + (head[n] >= 0).astype(jnp.int32)

        found = lax.fori_loop(0, tiles, name, jnp.int32(0))

        def columns(s):
            return block(coords[lax.rem(s + core * local, slots), 0], tile)

        def two_slots(s):
            t = link[s]
            there = t >= 0
            t = jnp.maximum(t, 0)
            a = jnp.concatenate([factor[rows, columns(s)], factor[rows, columns(t)]], axis=1)
            b = jnp.concatenate([held[s], jnp.where(there, held[t], jnp.zeros_like(held[t]))], axis=0)
            return jnp.dot(a, b, preferred_element_type=jnp.float32), jnp.where(there, link[t], -1)

        def one_tile(w, carry):
            s = starts[w]
            t = link[s]
            more = jnp.where(t >= 0, link[jnp.maximum(t, 0)], -1)
            here = block(w, tile)

            @pl.when(more < 0)
            def _():
                left[:, here] = two_slots(s)[0].astype(left.dtype)

            @pl.when(more >= 0)
            def _():
                value, after = two_slots(s)
                wide[...] = value

                def add(s):
                    value, after = two_slots(s)
                    wide[...] += value
                    return after

                lax.while_loop(lambda s: s >= 0, add, after)
                left[:, here] = wide[...].astype(left.dtype)

            return carry

        lax.fori_loop(0, found, one_tile, 0)

        @pl.when(lax.rem(found, 2) == 1)
        def _():
            left[:, block(found, tile)] = jnp.zeros((half, tile), left.dtype)
            names[found] = 0

        steps = (found + 1) // 2
        for n in range(1, tiles // 2 + 1):

            @pl.when(steps == n)
            def _():
                def piece(j, carry):
                    here = block(j, half)
                    right = jnp.concatenate(
                        [factor[here, block(names[u], tile)] for u in range(2 * n)], axis=1
                    )
                    value = lax.dot_general(
                        left[:, : n * span], right, LAST_LAST, preferred_element_type=jnp.float32
                    )
                    out[:, here] = value.astype(out.dtype)
                    return carry

                lax.fori_loop(0, width // half, piece, 0)

        @pl.when(steps == 0)
        def _():
            out[...] = jnp.zeros(out.shape, out.dtype)

    return pl.pallas_call(
        body,
        out_shape=jax.ShapeDtypeStruct((half, width), out_dtype),
        in_specs=[SMEM, SMEM, SMEM, VMEM, VMEM, VMEM],
        out_specs=VMEM,
        scratch_shapes=[
            pltpu.VMEM((half, tiles * tile), jnp.bfloat16),
            pltpu.VMEM((half, tile), jnp.float32),
            pltpu.VMEM((slots, tile, tile), jnp.bfloat16),
            pltpu.SMEM((tiles,), jnp.int32),
            pltpu.SMEM((slots,), jnp.int32),
            pltpu.SMEM((tiles + 1,), jnp.int32),
            pltpu.SMEM((tiles + 1,), jnp.int32),
        ],
        compiler_params=params(32),
        cost_estimate=pl.CostEstimate(
            flops=2 * half * width * width, bytes_accessed=2 * width * width, transcendentals=0
        ),
        name="ladder_far" if far else "ladder_near",
    )(coords, mask, place, own, other, factor)


def finish(orbs, place, sums, other_sums, near, arrived, cycle_factor, *, pieces):
    half, width = near.shape
    aux = cycle_factor.shape[2]
    share = sums.shape[0]
    rows = half // pieces

    def body(orbs, place, sums, other_sums, near, arrived, cycle_factor, out, low, factor, sem):
        step = pl.program_id(0)

        @pl.when(step == 0)
        def _():
            load = pltpu.make_async_copy(cycle_factor.at[orbs[0], block(place[0], half)], factor, sem)
            load.start()
            low[block(place[0], share), :] = sums[...]
            low[block(1 - place[0], share), :] = other_sums[...]
            load.wait()

        term = jnp.dot(factor[block(step, rows), :], low[...], preferred_element_type=jnp.float32)
        out[...] = (near[...].astype(jnp.float32) + arrived[...].astype(jnp.float32) + term).astype(out.dtype)

    piece = pl.BlockSpec((rows, width), lambda step: (step, 0))
    return pl.pallas_call(
        body,
        out_shape=jax.ShapeDtypeStruct((half, width), jnp.bfloat16),
        grid=(pieces,),
        in_specs=[SMEM, SMEM, VMEM, VMEM, piece, piece, ANY],
        out_specs=piece,
        scratch_shapes=[
            pltpu.VMEM((aux, width), jnp.bfloat16),
            pltpu.VMEM((half, aux), jnp.bfloat16),
            pltpu.SemaphoreType.DMA,
        ],
        compiler_params=params(32),
        name="finish",
    )(orbs, place, sums, other_sums, near, arrived, cycle_factor)


def shards(amp_tiles, tile_coords, tile_mask, pair_orbs, ladder_factor, cycle_factor):
    cores, pairs = lax.axis_size("virt"), lax.axis_size("pair")
    assert cores == 2 and pairs % 2 == 0
    own = amp_tiles[0]
    coords, mask, orbs = tile_coords[0], tile_mask[0], pair_orbs[0]
    place = lax.axis_index("virt").astype(jnp.int32).reshape(1)
    swap = [(0, 1), (1, 0)]
    other = lax.ppermute(own, "virt", swap)
    first, second = intermediate(coords, mask, orbs, place, own, other, cycle_factor, cores=cores)

    classes = pairs // 2
    far = [(p, (p + classes) % pairs) for p in range(pairs)]

    def shifts(value):
        return [
            lax.ppermute(
                value, "pair", [(p, p // classes * classes + (p + k) % classes) for p in range(pairs)]
            )
            for k in range(1, classes)
        ]

    if classes <= 4:
        first_far = lax.ppermute(first, "pair", far)
        second_near = shifts(second)
        first_sum, second_sum = sum_middle(first, first_far, second, second_near)
        second_sum_far = lax.ppermute(second_sum, "pair", far)
        sums = sum_last(second, second_near, first_sum, shifts(first_sum), second_sum, second_sum_far)
    else:
        width = first.shape[1]
        occupied = jnp.arange(cycle_factor.shape[0], dtype=jnp.int32) == orbs[1]
        mine = jnp.concatenate([first, second[:, :width]], axis=0).astype(jnp.float32)
        total = lax.psum(jnp.where(occupied[:, None, None], mine[None], 0.0), "pair")
        sums = lax.dynamic_index_in_dim(total, orbs[1], 0, keepdims=False).astype(jnp.bfloat16)

    factor = ladder_factor[0]
    outgoing = ladder(coords, mask, place, own, other, factor, far=True, out_dtype=jnp.bfloat16)
    arrived = lax.ppermute(outgoing, "virt", swap)
    near = ladder(coords, mask, place, own, other, factor, far=False, out_dtype=jnp.float32)
    other_sums = lax.ppermute(sums, "virt", swap)
    return finish(orbs, place, sums, other_sums, near, arrived, cycle_factor, pieces=4)[None]


def solution(mesh):
    in_specs = (
        P(("groups", "pair"), "virt", None, None),
        P(("groups", "pair"), None, None),
        P(("groups", "pair"), None),
        P(("groups", "pair"), None),
        P(("groups", "virt"), None, None),
        P("groups", None, None),
    )
    out_specs = P(("groups", "pair"), "virt", None)
    return jax.shard_map(shards, mesh=mesh, in_specs=in_specs, out_specs=out_specs, check_vma=False)
```

```python
import functools

import jax
import jax.numpy as jnp
from jax import lax
from jax.experimental import pallas as pl
from jax.experimental.pallas import tpu as pltpu
from jax.sharding import PartitionSpec as P

LANES = 128
SMEM = pl.BlockSpec(memory_space=pltpu.SMEM)
VMEM = pl.BlockSpec(memory_space=pltpu.VMEM)
HBM = pl.BlockSpec(memory_space=pltpu.HBM)
FIRST_FIRST = (((0,), (0,)), ((), ()))
LAST_LAST = (((1,), (1,)), ((), ()))
AFTER, COLUMN, ROW, KEPT, START, NAME, FACTS = range(7)
USED, CORE, ORBITAL = range(3)


def params(mib):
    return pltpu.CompilerParams(vmem_limit_bytes=mib * 2**20)


def block(index, size):
    return pl.ds(pl.multiple_of(index * size, size), size)


def in_hbm(array):
    return pltpu.with_memory_space_constraint(array, pltpu.HBM)


def in_smem(array):
    return pltpu.with_memory_space_constraint(array, pltpu.SMEM)


def add_terms(total, table, rows, tiles, slots):
    size = tiles.shape[1]
    terms = [
        lax.dot_general(
            rows[block(table[COLUMN, s], size), :], tiles[k], FIRST_FIRST, preferred_element_type=jnp.float32
        )
        for k, s in enumerate(slots)
    ]
    for s, term in zip(slots, terms):
        total[:, block(table[ROW, s], size)] += term * table[KEPT, s].astype(jnp.float32)


def prepare(coords, mask, orbs, place, own, cycle_factor):
    slots = coords.shape[1]
    local, tile = own.shape[0], own.shape[1]
    width, aux = cycle_factor.shape[1:]
    tiles = width // tile
    places = max(slots, -(-tiles // 4) * 4) + 1

    def body(coords, mask, orbs, place, own, factor, table, held, rows, total, s_coords, s_mask, s_orbs, head, sems):
        loads = [
            pltpu.make_async_copy(source, target, sems.at[n])
            for n, (source, target) in enumerate([(orbs, s_orbs), (coords, s_coords), (mask, s_mask), (own, held)])
        ]
        for load in loads:
            load.start()
        core = place[0]
        total[...] = jnp.zeros_like(total)
        loads[0].wait()
        load_rows = pltpu.make_async_copy(factor.at[s_orbs[0, 0]], rows, sems.at[4])
        load_rows.start()
        table[FACTS, CORE] = core
        table[FACTS, ORBITAL] = s_orbs[0, 1]

        def clear(n, carry):
            head[n] = slots
            table[START, n] = slots
            table[NAME, n] = 0
            return carry

        lax.fori_loop(0, places, clear, 0, unroll=True)
        table[AFTER, slots] = slots
        table[COLUMN, slots] = 0
        loads[1].wait()
        loads[2].wait()

        def put(s, carry):
            g = lax.rem(s + core * local, slots)
            d = s_coords[1, g]
            kept = s_mask[0, g]
            table[COLUMN, s] = s_coords[0, g]
            table[ROW, s] = d
            table[KEPT, s] = kept
            before = head[d]
            table[AFTER, s] = before
            head[d] = jnp.where(kept != 0, s, before)
            return carry

        lax.fori_loop(0, slots, put, 0, unroll=True)

        def name(n, count):
            first = head[n]
            table[NAME, count] = n
            table[START, count] = first
            return count + (first < slots).astype(jnp.int32)

        used = lax.fori_loop(0, tiles, name, jnp.int32(0), unroll=True)
        table[FACTS, USED] = used
        table[START, used] = slots
        table[NAME, used] = 0
        loads[3].wait()
        load_rows.wait()
        add_terms(total, table, rows, held, range(local))

    return pl.pallas_call(
        body,
        out_shape=[
            pltpu.SMEM((7, places), jnp.int32),
            jax.ShapeDtypeStruct(own.shape, own.dtype),
            jax.ShapeDtypeStruct((width, aux), jnp.bfloat16),
            jax.ShapeDtypeStruct((aux, width), jnp.float32),
        ],
        in_specs=[HBM, HBM, HBM, SMEM, HBM, HBM],
        out_specs=[SMEM, VMEM, VMEM, VMEM],
        scratch_shapes=[
            pltpu.SMEM(coords.shape, jnp.int32),
            pltpu.SMEM(mask.shape, jnp.int32),
            pltpu.SMEM(orbs.shape, jnp.int32),
            pltpu.SMEM((places,), jnp.int32),
            pltpu.SemaphoreType.DMA((5,)),
        ],
        compiler_params=params(16),
        name="prepare",
    )(in_hbm(coords), in_hbm(mask), in_hbm(orbs), place, in_hbm(own), in_hbm(cycle_factor))


def intermediate(table, own, other, rows, start, *, cores):
    local, tile = own.shape[0], own.shape[1]
    aux, width = start.shape
    share = aux // cores

    def body(table, own, other, rows, start, out, held, total):
        total[...] = start[...]
        add_terms(total, table, rows, other, range(local, 2 * local))
        out[:, :width] = total[block(table[FACTS, CORE], share), :].astype(out.dtype)
        label = jnp.zeros((share, LANES), jnp.float32) + table[FACTS, ORBITAL].astype(jnp.float32)
        out[:, width:] = label.astype(out.dtype)
        held[:local] = own[...]
        held[local : 2 * local] = other[...]
        held[2 * local] = jnp.zeros((tile, tile), held.dtype)

    return pl.pallas_call(
        body,
        out_shape=[
            jax.ShapeDtypeStruct((share, width + LANES), jnp.bfloat16),
            jax.ShapeDtypeStruct((2 * local + 1, tile, tile), jnp.bfloat16),
        ],
        in_specs=[SMEM, VMEM, VMEM, VMEM, VMEM],
        out_specs=[VMEM, VMEM],
        scratch_shapes=[pltpu.VMEM((aux, width), jnp.float32)],
        compiler_params=params(16),
        name="intermediate",
    )(in_smem(table), own, other, rows, start)


def add_arrivals(table, mine, arrivals, *, plain, labelled):
    share, full = mine.shape
    width = full - LANES

    def body(table, mine, *refs):
        arrivals, out = refs[:-1], refs[-1]
        total = mine[:, :width].astype(jnp.float32)
        label = mine[:, width : width + 1].astype(jnp.float32)
        as_is = table[FACTS, CORE] == plain
        for k, theirs in enumerate(arrivals):
            same = (label == theirs[:, width : width + 1].astype(jnp.float32)).astype(jnp.float32)
            weight = jnp.where(as_is, float(k == len(arrivals) - 1), same)
            total += jnp.where(weight > 0.5, theirs[:, :width].astype(jnp.float32), 0.0)
        out[:, :width] = total.astype(out.dtype)
        if labelled:
            out[:, width:] = mine[:, width:]

    return pl.pallas_call(
        body,
        out_shape=jax.ShapeDtypeStruct((share, full if labelled else width), mine.dtype),
        in_specs=[SMEM, VMEM] + [VMEM] * len(arrivals),
        out_specs=VMEM,
        compiler_params=params(16),
        name="sum_middle" if labelled else "sum_last",
    )(in_smem(table), mine, *arrivals)


def ladder(table, held, factor, *, far, out_dtype):
    empty, tile = held.shape[0] - 1, held.shape[1]
    width = factor.shape[0]
    half = width // 2
    tiles = width // tile
    span = 2 * tile
    group = 4
    room = -(-tiles // group) * group

    def body(table, held, factor, out, left, wide):
        core = table[FACTS, CORE]
        rows = block(1 - core if far else core, half)
        found = table[FACTS, USED]

        def two_slots(s):
            t = table[AFTER, s]
            a = jnp.concatenate(
                [factor[rows, block(table[COLUMN, s], tile)], factor[rows, block(table[COLUMN, t], tile)]], axis=1
            )
            b = jnp.concatenate([held[s], held[t]], axis=0)
            return jnp.dot(a, b, preferred_element_type=jnp.float32), table[AFTER, t]

        def some_tiles(m, carry):
            for k in range(group):
                w = m * group + k
                left[:, block(w, tile)] = two_slots(table[START, w])[0].astype(left.dtype)
            return carry

        lax.fori_loop(0, (found + group - 1) // group, some_tiles, 0)

        def long_tile(w, carry):
            s = table[START, w]

            @pl.when(table[AFTER, table[AFTER, s]] != empty)
            def _():
                value, after = two_slots(s)
                wide[...] = value

                def add(s):
                    value, after = two_slots(s)
                    wide[...] += value
                    return after

                lax.while_loop(lambda s: s != empty, add, after)
                left[:, block(w, tile)] = wide[...].astype(left.dtype)

            return carry

        lax.fori_loop(0, found, long_tile, 0)

        steps = (found + 1) // 2
        for n in range(1, tiles // 2 + 1):

            @pl.when(steps == n)
            def _():
                def piece(j, carry):
                    here = block(j, half)
                    right = jnp.concatenate(
                        [factor[here, block(table[NAME, u], tile)] for u in range(2 * n)], axis=1
                    )
                    value = lax.dot_general(
                        left[:, : n * span], right, LAST_LAST, preferred_element_type=jnp.float32
                    )
                    out[:, here] = value.astype(out.dtype)
                    return carry

                lax.fori_loop(0, width // half, piece, 0)

        @pl.when(steps == 0)
        def _():
            out[...] = jnp.zeros(out.shape, out.dtype)

    return pl.pallas_call(
        body,
        out_shape=jax.ShapeDtypeStruct((half, width), out_dtype),
        in_specs=[SMEM, VMEM, VMEM],
        out_specs=VMEM,
        scratch_shapes=[
            pltpu.VMEM((half, room * tile), jnp.bfloat16),
            pltpu.VMEM((half, tile), jnp.float32),
        ],
        compiler_params=params(32),
        cost_estimate=pl.CostEstimate(
            flops=2 * half * width * width, bytes_accessed=2 * width * width, transcendentals=0
        ),
        name="ladder_far" if far else "ladder_near",
    )(in_smem(table), held, factor)


def finish(table, sums, other_sums, near, arrived, cycle_rows, *, pieces):
    half, width = near.shape
    aux = cycle_rows.shape[1]
    share = sums.shape[0]
    rows = half // pieces

    def body(table, sums, other_sums, near, arrived, factor, out, low, done, sems):
        core = table[FACTS, CORE]
        low[block(core, share), :] = sums[...]
        low[block(1 - core, share), :] = other_sums[...]
        stores = []
        for n in range(pieces):
            here = slice(n * rows, (n + 1) * rows)
            term = jnp.dot(
                factor[pl.ds(pl.multiple_of(core * half + n * rows, rows), rows), :], low[...],
                preferred_element_type=jnp.float32,
            )
            done[here, :] = (near[here, :].astype(jnp.float32) + arrived[here, :].astype(jnp.float32) + term).astype(done.dtype)
            store = pltpu.make_async_copy(done.at[here, :], out.at[here, :], sems.at[n])
            store.start()
            stores.append(store)
        for store in stores:
            store.wait()

    return pl.pallas_call(
        body,
        out_shape=jax.ShapeDtypeStruct((half, width), jnp.bfloat16),
        in_specs=[SMEM, VMEM, VMEM, VMEM, VMEM, VMEM],
        out_specs=HBM,
        scratch_shapes=[
            pltpu.VMEM((aux, width), jnp.bfloat16),
            pltpu.VMEM((half, width), jnp.bfloat16),
            pltpu.SemaphoreType.DMA((pieces,)),
        ],
        compiler_params=params(32),
        name="finish",
    )(in_smem(table), sums, other_sums, near, arrived, cycle_rows)


def shards(amp_tiles, tile_coords, tile_mask, pair_orbs, ladder_factor, cycle_factor):
    cores, pairs = lax.axis_size("virt"), lax.axis_size("pair")
    assert cores == 2 and pairs % 2 == 0
    own = amp_tiles[0]
    place = lax.axis_index("virt").astype(jnp.int32).reshape(1)
    swap = [(0, 1), (1, 0)]
    other = lax.ppermute(own, "virt", swap)
    table, own, cycle_rows, start = prepare(tile_coords[0].T, tile_mask, pair_orbs, place, own, cycle_factor)
    message, held = intermediate(table, own, other, cycle_rows, start, cores=cores)
    factor = ladder_factor[0]
    outgoing = ladder(table, held, factor, far=True, out_dtype=jnp.bfloat16)

    classes = pairs // 2
    even = classes & (classes - 1) == 0

    def within(p, k):
        return p // classes * classes + (p % classes ^ k if even else (p % classes + k) % classes)

    def permute(value, k, far_core):
        routes = []
        for p in range(pairs):
            for core in range(cores):
                if core != far_core:
                    routes.append((p * cores + core, within(p, k) * cores + core))
                elif k == classes - 1:
                    routes.append((p * cores + core, (p + classes) % pairs * cores + core))
        return lax.ppermute(value, ("pair", "virt"), routes)

    if 2 <= classes <= 4:
        arrivals = [permute(message, k, 0) for k in range(1, classes)]
        arrivals, outgoing = lax.optimization_barrier((arrivals, outgoing))
        arrived = lax.ppermute(outgoing, "virt", swap)
        middle = add_arrivals(table, message, arrivals, plain=0, labelled=True)
        middle, held = lax.optimization_barrier((middle, held))
        near = ladder(table, held, factor, far=False, out_dtype=jnp.float32)
        arrivals = [permute(middle, k, 1) for k in range(1, classes)]
        arrivals, near = lax.optimization_barrier((arrivals, near))
        sums = add_arrivals(table, middle, arrivals, plain=1, labelled=False)
    else:
        arrived = lax.ppermute(outgoing, "virt", swap)
        near = ladder(table, held, factor, far=False, out_dtype=jnp.float32)
        width = factor.shape[0]
        right = pair_orbs[0, 1]
        occupied = jnp.arange(cycle_factor.shape[0], dtype=jnp.int32) == right
        mine = message[:, :width].astype(jnp.float32)
        total = lax.psum(jnp.where(occupied[:, None, None], mine[None], 0.0), "pair")
        sums = lax.dynamic_index_in_dim(total, right, 0, keepdims=False).astype(jnp.bfloat16)

    other_sums = lax.ppermute(sums, "virt", swap)
    return finish(table, sums, other_sums, near, arrived, cycle_rows, pieces=4)[None]


def solution(mesh):
    in_specs = (
        P(("groups", "pair"), "virt", None, None),
        P(("groups", "pair"), None, None),
        P(("groups", "pair"), None),
        P(("groups", "pair"), None),
        P(("groups", "virt"), None, None),
        P("groups", None, None),
    )
    out_specs = P(("groups", "pair"), "virt", None)
    return jax.shard_map(shards, mesh=mesh, in_specs=in_specs, out_specs=out_specs, check_vma=False)
```

```python
import functools

import jax
import jax.numpy as jnp
from jax import lax
from jax.experimental import pallas as pl
from jax.experimental.pallas import tpu as pltpu
from jax.sharding import PartitionSpec as P

LANES = 128
SMEM = pl.BlockSpec(memory_space=pltpu.SMEM)
VMEM = pl.BlockSpec(memory_space=pltpu.VMEM)
HBM = pl.BlockSpec(memory_space=pltpu.HBM)
FIRST_FIRST = (((0,), (0,)), ((), ()))
LAST_LAST = (((1,), (1,)), ((), ()))
AFTER, COLUMN, ROW, KEPT, START, NAME, FACTS = range(7)
USED, CORE, ORBITAL = range(3)


def params(mib):
    return pltpu.CompilerParams(vmem_limit_bytes=mib * 2**20)


def block(index, size):
    return pl.ds(pl.multiple_of(index * size, size), size)


def in_hbm(array):
    return pltpu.with_memory_space_constraint(array, pltpu.HBM)


def in_smem(array):
    return pltpu.with_memory_space_constraint(array, pltpu.SMEM)


def add_terms(total, table, rows, tiles, slots):
    size = tiles.shape[1]
    terms = [
        lax.dot_general(
            rows[block(table[COLUMN, s], size), :], tiles[k], FIRST_FIRST, preferred_element_type=jnp.float32
        )
        for k, s in enumerate(slots)
    ]
    for s, term in zip(slots, terms):
        total[:, block(table[ROW, s], size)] += term * table[KEPT, s].astype(jnp.float32)


def prepare(coords, mask, orbs, place, own, cycle_factor):
    slots = coords.shape[1]
    local, tile = own.shape[0], own.shape[1]
    width, aux = cycle_factor.shape[1:]
    tiles = width // tile
    places = max(slots, -(-tiles // 4) * 4) + 1

    def body(coords, mask, orbs, place, own, factor, table, held, rows, total, s_coords, s_mask, s_orbs, head, sems):
        loads = [
            pltpu.make_async_copy(source, target, sems.at[n])
            for n, (source, target) in enumerate([(orbs, s_orbs), (coords, s_coords), (mask, s_mask), (own, held)])
        ]
        for load in loads:
            load.start()
        core = place[0]
        total[...] = jnp.zeros_like(total)
        loads[0].wait()
        load_rows = pltpu.make_async_copy(factor.at[s_orbs[0, 0]], rows, sems.at[4])
        load_rows.start()
        table[FACTS, CORE] = core
        table[FACTS, ORBITAL] = s_orbs[0, 1]

        def clear(n, carry):
            head[n] = slots
            table[START, n] = slots
            table[NAME, n] = 0
            return carry

        lax.fori_loop(0, places, clear, 0, unroll=True)
        table[AFTER, slots] = slots
        table[COLUMN, slots] = 0
        loads[1].wait()
        loads[2].wait()

        def put(s, carry):
            g = lax.rem(s + core * local, slots)
            d = s_coords[1, g]
            kept = s_mask[0, g]
            table[COLUMN, s] = s_coords[0, g]
            table[ROW, s] = d
            table[KEPT, s] = kept
            before = head[d]
            table[AFTER, s] = before
            head[d] = jnp.where(kept != 0, s, before)
            return carry

        lax.fori_loop(0, slots, put, 0, unroll=True)

        def name(n, count):
            first = head[n]
            table[NAME, count] = n
            table[START, count] = first
            return count + (first < slots).astype(jnp.int32)

        used = lax.fori_loop(0, tiles, name, jnp.int32(0), unroll=True)
        table[FACTS, USED] = used
        table[START, used] = slots
        table[NAME, used] = 0
        loads[3].wait()
        load_rows.wait()
        add_terms(total, table, rows, held, range(local))

    return pl.pallas_call(
        body,
        out_shape=[
            pltpu.SMEM((7, places), jnp.int32),
            jax.ShapeDtypeStruct(own.shape, own.dtype),
            jax.ShapeDtypeStruct((width, aux), jnp.bfloat16),
            jax.ShapeDtypeStruct((aux, width), jnp.float32),
        ],
        in_specs=[HBM, HBM, HBM, SMEM, HBM, HBM],
        out_specs=[SMEM, VMEM, VMEM, VMEM],
        scratch_shapes=[
            pltpu.SMEM(coords.shape, jnp.int32),
            pltpu.SMEM(mask.shape, jnp.int32),
            pltpu.SMEM(orbs.shape, jnp.int32),
            pltpu.SMEM((places,), jnp.int32),
            pltpu.SemaphoreType.DMA((5,)),
        ],
        compiler_params=params(16),
        name="prepare",
    )(in_hbm(coords), in_hbm(mask), in_hbm(orbs), place, in_hbm(own), in_hbm(cycle_factor))


def intermediate(table, own, other, rows, start, *, cores):
    local, tile = own.shape[0], own.shape[1]
    aux, width = start.shape
    share = aux // cores

    def body(table, own, other, rows, start, out, held, total):
        total[...] = start[...]
        add_terms(total, table, rows, other, range(local, 2 * local))
        out[:, :width] = total[block(table[FACTS, CORE], share), :].astype(out.dtype)
        label = jnp.zeros((share, LANES), jnp.float32) + table[FACTS, ORBITAL].astype(jnp.float32)
        out[:, width:] = label.astype(out.dtype)
        held[:local] = own[...]
        held[local : 2 * local] = other[...]
        held[2 * local] = jnp.zeros((tile, tile), held.dtype)

    return pl.pallas_call(
        body,
        out_shape=[
            jax.ShapeDtypeStruct((share, width + LANES), jnp.bfloat16),
            jax.ShapeDtypeStruct((2 * local + 1, tile, tile), jnp.bfloat16),
        ],
        in_specs=[SMEM, VMEM, VMEM, VMEM, VMEM],
        out_specs=[VMEM, VMEM],
        scratch_shapes=[pltpu.VMEM((aux, width), jnp.float32)],
        compiler_params=params(16),
        name="intermediate",
    )(in_smem(table), own, other, rows, start)


def step(table, next_orbs, mine, arrival, *, plain):
    share, full = arrival.shape
    width = full - LANES

    def body(table, next_orbs, mine, arrival, kept, out):
        value = mine[:, :width].astype(jnp.float32)
        extra = arrival[:, :width].astype(jnp.float32)
        own = jnp.zeros((share, LANES), jnp.float32) + table[FACTS, ORBITAL].astype(jnp.float32)
        out[:, width:] = own.astype(out.dtype)

        @pl.when(table[FACTS, CORE] == plain)
        def _():
            total = value + extra
            kept[...] = total
            out[:, :width] = total.astype(out.dtype)

        @pl.when(table[FACTS, CORE] != plain)
        def _():
            label = own[:, :1]
            theirs = arrival[:, width : width + 1].astype(jnp.float32)
            behind = next_orbs[0:1, 1:2].astype(jnp.float32)
            kept[...] = value + jnp.where(theirs == label, extra, 0.0)
            out[:, :width] = (
                jnp.where(label == behind, value, 0.0) + jnp.where(theirs == behind, extra, 0.0)
            ).astype(out.dtype)

    return pl.pallas_call(
        body,
        out_shape=[
            jax.ShapeDtypeStruct((share, width), jnp.float32),
            jax.ShapeDtypeStruct((share, full), arrival.dtype),
        ],
        in_specs=[SMEM, VMEM, VMEM, VMEM],
        out_specs=[VMEM, VMEM],
        compiler_params=params(16),
        name="step",
    )(in_smem(table), next_orbs, mine, arrival)


def last_step(mine, arrival):
    width = mine.shape[1]

    def body(mine, arrival, out):
        out[...] = (mine[...] + arrival[:, :width].astype(jnp.float32)).astype(out.dtype)

    return pl.pallas_call(
        body,
        out_shape=jax.ShapeDtypeStruct(mine.shape, arrival.dtype),
        in_specs=[VMEM, VMEM],
        out_specs=VMEM,
        compiler_params=params(16),
        name="last_step",
    )(mine, arrival)


def build_half(table, held, factor, left, wide, *, far):
    empty, tile = held.shape[0] - 1, held.shape[1]
    half, group = left.shape[0], 4
    core = table[FACTS, CORE]
    found = table[FACTS, USED]
    rows = block(1 - core if far else core, half)

    def two_slots(s):
        t = table[AFTER, s]
        a = jnp.concatenate(
            [factor[rows, block(table[COLUMN, s], tile)], factor[rows, block(table[COLUMN, t], tile)]], axis=1
        )
        b = jnp.concatenate([held[s], held[t]], axis=0)
        return jnp.dot(a, b, preferred_element_type=jnp.float32), table[AFTER, t]

    def some_tiles(m, carry):
        for k in range(group):
            w = m * group + k
            left[:, block(w, tile)] = two_slots(table[START, w])[0].astype(left.dtype)
        return carry

    lax.fori_loop(0, (found + group - 1) // group, some_tiles, 0)

    def long_tile(w, carry):
        s = table[START, w]

        @pl.when(table[AFTER, table[AFTER, s]] != empty)
        def _():
            value, after = two_slots(s)
            wide[...] = value

            def add(s):
                value, after = two_slots(s)
                wide[...] += value
                return after

            lax.while_loop(lambda s: s != empty, add, after)
            left[:, block(w, tile)] = wide[...].astype(left.dtype)

        return carry

    lax.fori_loop(0, found, long_tile, 0)


def multiply(table, left, factor, tile, first_side, out):
    half = left.shape[0]
    steps = (table[FACTS, USED] + 1) // 2
    for n in range(factor.shape[0] // tile // 2 + 1):

        @pl.when(steps == n)
        def _():
            def unit(k, carry):
                if n == 0:
                    out[k] = jnp.zeros((half, half), out.dtype)
                    return carry
                here = block(first_side + k, half)
                right = jnp.concatenate(
                    [factor[here, block(table[NAME, w], tile)] for w in range(2 * n)], axis=1
                )
                out[k] = lax.dot_general(
                    left[:, : 2 * n * tile], right, LAST_LAST, preferred_element_type=jnp.float32
                ).astype(out.dtype)
                return carry

            lax.fori_loop(0, out.shape[0], unit, 0)


def ladder_first(table, held, factor):
    tile = held.shape[1]
    width = factor.shape[0]
    half = width // 2
    room = -(-(width // tile) // 4) * 4 * tile

    def body(table, held, factor, left, far_a, wide):
        build_half(table, held, factor, left, wide, far=True)
        multiply(table, left, factor, tile, 0, far_a)

    return ladder_call(
        body, [(half, room), (1, half, half)], (half, tile), in_smem(table), held, factor, flops=10**10
    )


def ladder_second(table, held, factor, left_far):
    tile = held.shape[1]
    half, room = left_far.shape

    def body(table, held, factor, left_far, left, far_b, wide):
        multiply(table, left_far, factor, tile, 1, far_b)
        build_half(table, held, factor, left, wide, far=False)

    return ladder_call(
        body, [(half, room), (1, half, half)], (half, tile), in_smem(table), held, factor, left_far, flops=10**10
    )


def ladder_third(table, factor, left, tile):
    half = left.shape[0]

    def body(table, factor, left, near, wide):
        multiply(table, left, factor, tile, 0, near)

    return ladder_call(body, [(2, half, half)], (half, tile), in_smem(table), factor, left, flops=4 * 10**10)[0]


def ladder_call(body, shapes, wide, *operands, flops):
    return pl.pallas_call(
        body,
        out_shape=[jax.ShapeDtypeStruct(shape, jnp.bfloat16) for shape in shapes],
        in_specs=[SMEM] + [VMEM] * (len(operands) - 1),
        out_specs=[VMEM] * len(shapes),
        scratch_shapes=[pltpu.VMEM(wide, jnp.float32)],
        compiler_params=params(32),
        cost_estimate=pl.CostEstimate(flops=flops, bytes_accessed=1, transcendentals=0),
        name="ladder",
    )(*operands)


def finish(table, sums, other_sums, near, arrived, cycle_rows, *, pieces):
    half, width = near.shape[1], 2 * near.shape[2]
    aux = cycle_rows.shape[1]
    share = sums.shape[0]
    rows = half // pieces

    def body(table, sums, other_sums, near, far_a, far_b, factor, out, low, done, sems):
        core = table[FACTS, CORE]
        low[block(core, share), :] = sums[...]
        low[block(1 - core, share), :] = other_sums[...]
        stores = []
        for n in range(pieces):
            here = slice(n * rows, (n + 1) * rows)
            term = jnp.dot(
                factor[pl.ds(pl.multiple_of(core * half + n * rows, rows), rows), :], low[...],
                preferred_element_type=jnp.float32,
            )
            for k, arrived in enumerate([far_a, far_b]):
                side = slice(k * half, (k + 1) * half)
                total = near[k, here, :].astype(jnp.float32) + arrived[0, here, :].astype(jnp.float32) + term[:, side]
                done[here, side] = total.astype(done.dtype)
            store = pltpu.make_async_copy(done.at[here, :], out.at[here, :], sems.at[n])
            store.start()
            stores.append(store)
        for store in stores:
            store.wait()

    return pl.pallas_call(
        body,
        out_shape=jax.ShapeDtypeStruct((half, width), jnp.bfloat16),
        in_specs=[SMEM] + [VMEM] * 6,
        out_specs=HBM,
        scratch_shapes=[
            pltpu.VMEM((aux, width), jnp.bfloat16),
            pltpu.VMEM((half, width), jnp.bfloat16),
            pltpu.SemaphoreType.DMA((pieces,)),
        ],
        compiler_params=params(32),
        name="finish",
    )(in_smem(table), sums, other_sums, near, *arrived, cycle_rows)


def shards(amp_tiles, tile_coords, tile_mask, pair_orbs, ladder_factor, cycle_factor):
    cores, pairs = lax.axis_size("virt"), lax.axis_size("pair")
    assert cores == 2 and pairs % 2 == 0
    own = amp_tiles[0]
    place = lax.axis_index("virt").astype(jnp.int32).reshape(1)
    swap = [(0, 1), (1, 0)]
    other = lax.ppermute(own, "virt", swap)
    square = pairs == 8
    if square:
        next_orbs = lax.ppermute(pair_orbs, "pair", [(p, p ^ 2) for p in range(pairs)])
    table, own, cycle_rows, start = prepare(tile_coords[0].T, tile_mask, pair_orbs, place, own, cycle_factor)
    message, held = intermediate(table, own, other, cycle_rows, start, cores=cores)
    factor = ladder_factor[0]

    def exchange(value, first_core, second_core):
        partners = (first_core, second_core)
        routes = [(p * 2 + c, (p ^ partners[c]) * 2 + c) for p in range(pairs) for c in range(2)]
        return lax.ppermute(value, ("pair", "virt"), routes)

    if square:
        arrival = exchange(message, 4, 1)
        left, far_a = ladder_first(table, held, factor)
        arrival, left = lax.optimization_barrier((arrival, left))
        kept, message = step(table, next_orbs, message, arrival, plain=0)
        message, left = lax.optimization_barrier((message, left))
        arrival = exchange(message, 1, 2)
        left, far_b = ladder_second(table, held, factor, left)
        arrival, left = lax.optimization_barrier((arrival, left))
        kept, message = step(table, next_orbs, kept, arrival, plain=1)
        message, left, far_a, far_b = lax.optimization_barrier((message, left, far_a, far_b))
        arrival = exchange(message, 2, 4)
        arrived = [lax.ppermute(far, "virt", swap) for far in (far_a, far_b)]
        near = ladder_third(table, factor, left, held.shape[1])
        arrival, near = lax.optimization_barrier((arrival, near))
        sums = last_step(kept, arrival)
    else:
        left, far_a = ladder_first(table, held, factor)
        left, far_b = ladder_second(table, held, factor, left)
        near = ladder_third(table, factor, left, held.shape[1])
        arrived = [lax.ppermute(far, "virt", swap) for far in (far_a, far_b)]
        width = factor.shape[0]
        right = pair_orbs[0, 1]
        occupied = jnp.arange(cycle_factor.shape[0], dtype=jnp.int32) == right
        mine = message[:, :width].astype(jnp.float32)
        total = lax.psum(jnp.where(occupied[:, None, None], mine[None], 0.0), "pair")
        sums = lax.dynamic_index_in_dim(total, right, 0, keepdims=False).astype(jnp.bfloat16)

    other_sums = lax.ppermute(sums, "virt", swap)
    return finish(table, sums, other_sums, near, arrived, cycle_rows, pieces=4)[None]


def solution(mesh):
    in_specs = (
        P(("groups", "pair"), "virt", None, None),
        P(("groups", "pair"), None, None),
        P(("groups", "pair"), None),
        P(("groups", "pair"), None),
        P(("groups", "virt"), None, None),
        P("groups", None, None),
    )
    out_specs = P(("groups", "pair"), "virt", None)
    return jax.shard_map(shards, mesh=mesh, in_specs=in_specs, out_specs=out_specs, check_vma=False)
```

```python
import functools

import jax
import jax.numpy as jnp
from jax import lax
from jax.experimental import pallas as pl
from jax.experimental.pallas import tpu as pltpu
from jax.sharding import PartitionSpec as P

LANES = 128
SMEM = pl.BlockSpec(memory_space=pltpu.SMEM)
VMEM = pl.BlockSpec(memory_space=pltpu.VMEM)
HBM = pl.BlockSpec(memory_space=pltpu.HBM)
FIRST_FIRST = (((0,), (0,)), ((), ()))
LAST_LAST = (((1,), (1,)), ((), ()))
COLUMN, ROW, KEPT, SORTED, NAME, BEGIN, FACTS = range(7)
USED, CORE, ORBITAL = range(3)


def params(mib):
    return pltpu.CompilerParams(vmem_limit_bytes=mib * 2**20)


def block(index, size):
    return pl.ds(pl.multiple_of(index * size, size), size)


def in_hbm(array):
    return pltpu.with_memory_space_constraint(array, pltpu.HBM)


def in_smem(array):
    return pltpu.with_memory_space_constraint(array, pltpu.SMEM)


def add_terms(total, table, rows, tiles, slots):
    size = tiles.shape[1]
    terms = [
        lax.dot_general(
            rows[block(table[COLUMN, s], size), :], tiles[k], FIRST_FIRST, preferred_element_type=jnp.float32
        )
        for k, s in enumerate(slots)
    ]
    for s, term in zip(slots, terms):
        total[:, block(table[ROW, s], size)] += term * table[KEPT, s].astype(jnp.float32)


def prepare(coords, mask, orbs, place, own, cycle_factor):
    slots = coords.shape[1]
    local, tile = own.shape[0], own.shape[1]
    width, aux = cycle_factor.shape[1:]
    tiles = width // tile
    places = max(slots + 1, tiles + 3)

    def body(coords, mask, orbs, place, own, factor, table, held, rows, total, s_coords, s_mask, s_orbs, count, sems):
        loads = [
            pltpu.make_async_copy(source, target, sems.at[n])
            for n, (source, target) in enumerate([(orbs, s_orbs), (coords, s_coords), (mask, s_mask), (own, held)])
        ]
        for load in loads:
            load.start()
        core = place[0]
        total[...] = jnp.zeros_like(total)
        loads[0].wait()
        load_rows = pltpu.make_async_copy(factor.at[s_orbs[0, 0]], rows, sems.at[4])
        load_rows.start()
        table[FACTS, CORE] = core
        table[FACTS, ORBITAL] = s_orbs[0, 1]

        for n in range(tiles):
            count[n] = 0
        loads[1].wait()
        loads[2].wait()
        for s in range(slots):
            g = lax.rem(s + core * local, slots)
            d, kept = s_coords[1, g], s_mask[0, g]
            table[COLUMN, s] = s_coords[0, g]
            table[ROW, s] = d
            table[KEPT, s] = kept
            table[SORTED, s] = slots
            count[d] += (kept != 0).astype(jnp.int32)
        table[COLUMN, slots] = 0
        begin, used = jnp.int32(0), jnp.int32(0)
        for n in range(tiles):
            here = count[n]
            table[NAME, used] = n
            table[BEGIN, used] = begin
            count[n] = begin
            begin += here
            used += (here > 0).astype(jnp.int32)
        table[FACTS, USED] = used
        for n in range(3):
            table[NAME, used + n] = 0
            table[BEGIN, used + n] = begin
        for s in range(slots):
            d = table[ROW, s]
            at = count[d]
            kept = table[KEPT, s] != 0
            table[SORTED, jnp.where(kept, at, slots)] = s
            count[d] = at + kept.astype(jnp.int32)
        loads[3].wait()
        load_rows.wait()
        add_terms(total, table, rows, held, range(local))

    return pl.pallas_call(
        body,
        out_shape=[
            pltpu.SMEM((7, places), jnp.int32),
            jax.ShapeDtypeStruct(own.shape, own.dtype),
            jax.ShapeDtypeStruct((width, aux), jnp.bfloat16),
            jax.ShapeDtypeStruct((aux, width), jnp.float32),
        ],
        in_specs=[HBM, HBM, HBM, SMEM, HBM, HBM],
        out_specs=[SMEM, VMEM, VMEM, VMEM],
        scratch_shapes=[
            pltpu.SMEM(coords.shape, jnp.int32),
            pltpu.SMEM(mask.shape, jnp.int32),
            pltpu.SMEM(orbs.shape, jnp.int32),
            pltpu.SMEM((tiles,), jnp.int32),
            pltpu.SemaphoreType.DMA((5,)),
        ],
        compiler_params=params(16),
        name="prepare",
    )(in_hbm(coords), in_hbm(mask), in_hbm(orbs), place, in_hbm(own), in_hbm(cycle_factor))


def intermediate(table, own, other, rows, start, *, cores):
    local, tile = own.shape[0], own.shape[1]
    aux, width = start.shape
    share = aux // cores

    def body(table, own, other, rows, start, out, held, total):
        total[...] = start[...]
        add_terms(total, table, rows, other, range(local, 2 * local))
        out[:, :width] = total[block(table[FACTS, CORE], share), :].astype(out.dtype)
        label = jnp.zeros((share, LANES), jnp.float32) + table[FACTS, ORBITAL].astype(jnp.float32)
        out[:, width:] = label.astype(out.dtype)
        held[:local] = own[...]
        held[local : 2 * local] = other[...]
        held[2 * local] = jnp.zeros((tile, tile), held.dtype)

    return pl.pallas_call(
        body,
        out_shape=[
            jax.ShapeDtypeStruct((share, width + LANES), jnp.bfloat16),
            jax.ShapeDtypeStruct((2 * local + 1, tile, tile), jnp.bfloat16),
        ],
        in_specs=[SMEM, VMEM, VMEM, VMEM, VMEM],
        out_specs=[VMEM, VMEM],
        scratch_shapes=[pltpu.VMEM((aux, width), jnp.float32)],
        compiler_params=params(16),
        name="intermediate",
    )(in_smem(table), own, other, rows, start)


def step(table, next_orbs, mine, arrival, *, plain):
    share, full = arrival.shape
    width = full - LANES

    def body(table, next_orbs, mine, arrival, kept, out):
        value = mine[:, :width].astype(jnp.float32)
        extra = arrival[:, :width].astype(jnp.float32)
        own = jnp.zeros((share, LANES), jnp.float32) + table[FACTS, ORBITAL].astype(jnp.float32)
        out[:, width:] = own.astype(out.dtype)

        @pl.when(table[FACTS, CORE] == plain)
        def _():
            total = value + extra
            kept[...] = total
            out[:, :width] = total.astype(out.dtype)

        @pl.when(table[FACTS, CORE] != plain)
        def _():
            label = own[:, :1]
            theirs = arrival[:, width : width + 1].astype(jnp.float32)
            behind = next_orbs[0:1, 1:2].astype(jnp.float32)
            kept[...] = value + jnp.where(theirs == label, extra, 0.0)
            out[:, :width] = (
                jnp.where(label == behind, value, 0.0) + jnp.where(theirs == behind, extra, 0.0)
            ).astype(out.dtype)

    return pl.pallas_call(
        body,
        out_shape=[
            jax.ShapeDtypeStruct((share, width), jnp.float32),
            jax.ShapeDtypeStruct((share, full), arrival.dtype),
        ],
        in_specs=[SMEM, VMEM, VMEM, VMEM],
        out_specs=[VMEM, VMEM],
        compiler_params=params(16),
        name="step",
    )(in_smem(table), next_orbs, mine, arrival)


def last_step(mine, arrival):
    width = mine.shape[1]

    def body(mine, arrival, out):
        out[...] = (mine[...] + arrival[:, :width].astype(jnp.float32)).astype(out.dtype)

    return pl.pallas_call(
        body,
        out_shape=jax.ShapeDtypeStruct(mine.shape, arrival.dtype),
        in_specs=[VMEM, VMEM],
        out_specs=VMEM,
        compiler_params=params(16),
        name="last_step",
    )(mine, arrival)


def ladder_build(table, held, factor):
    empty, tile = held.shape[0] - 1, held.shape[1]
    width = factor.shape[0]
    pairs = -(-(width // tile) // 2)

    def body(table, held, factor, left, wide):
        def two_tiles(m, carry):
            first, second, end = [table[BEGIN, 2 * m + k] for k in range(3)]
            here = block(m, 2 * tile)

            def product(at, count):
                columns, weights = [], []
                for k in range(count):
                    s = jnp.where(at + k < end, table[SORTED, jnp.minimum(at + k, empty)], empty)
                    columns.append(factor[:, block(table[COLUMN, s], tile)])
                    value, none = held[s], jnp.zeros((tile, tile), held.dtype)
                    early = at + k < second
                    weights.append(
                        jnp.concatenate([jnp.where(early, value, none), jnp.where(early, none, value)], axis=1)
                    )
                return jnp.dot(
                    jnp.concatenate(columns, axis=1), jnp.concatenate(weights, axis=0),
                    preferred_element_type=jnp.float32,
                )

            rounds = (end - first + 1) // 2
            for n in range(1, 4):

                @pl.when(rounds == n)
                def _():
                    left[:, here] = product(first, 2 * n).astype(left.dtype)

            @pl.when(rounds > 3)
            def _():
                wide[...] = product(first, 2)

                def add(t, carry):
                    wide[...] += product(first + 2 * t, 2)
                    return carry

                lax.fori_loop(1, rounds, add, 0)
                left[:, here] = wide[...].astype(left.dtype)

            return carry

        lax.fori_loop(0, (table[FACTS, USED] + 1) // 2, two_tiles, 0)

    wide = pltpu.VMEM((width, 2 * tile), jnp.float32)
    return ladder_call(body, (width, 2 * pairs * tile), [wide], in_smem(table), held, factor, flops=10**10)


def ladder_multiply(table, left, factor, tile, *, far, flops):
    half = left.shape[0] // 2

    def body(table, left, factor, out):
        core = table[FACTS, CORE]
        rows = block(1 - core if far else core, half)
        steps = (table[FACTS, USED] + 1) // 2
        for n in range(factor.shape[0] // tile // 2 + 1):

            @pl.when(steps == n)
            def _():
                def unit(k, carry):
                    if n == 0:
                        out[k] = jnp.zeros((half, half), out.dtype)
                        return carry
                    here = block(k, half)
                    right = jnp.concatenate(
                        [factor[here, block(table[NAME, w], tile)] for w in range(2 * n)], axis=1
                    )
                    out[k] = lax.dot_general(
                        left[rows, : 2 * n * tile], right, LAST_LAST, preferred_element_type=jnp.float32
                    ).astype(out.dtype)
                    return carry

                lax.fori_loop(0, 2, unit, 0)

    return ladder_call(body, (2, half, half), [], in_smem(table), left, factor, flops=flops)


def ladder_call(body, shape, scratch, *operands, flops):
    return pl.pallas_call(
        body,
        out_shape=jax.ShapeDtypeStruct(shape, jnp.bfloat16),
        in_specs=[SMEM] + [VMEM] * (len(operands) - 1),
        out_specs=VMEM,
        scratch_shapes=scratch,
        compiler_params=params(32),
        cost_estimate=pl.CostEstimate(flops=flops, bytes_accessed=1, transcendentals=0),
        name="ladder",
    )(*operands)


def finish(table, sums, other_sums, near, arrived, cycle_rows, *, pieces):
    half, width = near.shape[1], 2 * near.shape[2]
    aux = cycle_rows.shape[1]
    share = sums.shape[0]
    rows = half // pieces

    def body(table, sums, other_sums, near, arrived, factor, out, low, done, sems):
        core = table[FACTS, CORE]
        low[block(core, share), :] = sums[...]
        low[block(1 - core, share), :] = other_sums[...]
        stores = []
        for n in range(pieces):
            here = slice(n * rows, (n + 1) * rows)
            term = jnp.dot(
                factor[pl.ds(pl.multiple_of(core * half + n * rows, rows), rows), :], low[...],
                preferred_element_type=jnp.float32,
            )
            for k in range(2):
                side = slice(k * half, (k + 1) * half)
                total = near[k, here, :].astype(jnp.float32) + arrived[k, here, :].astype(jnp.float32) + term[:, side]
                done[here, side] = total.astype(done.dtype)
            store = pltpu.make_async_copy(done.at[here, :], out.at[here, :], sems.at[n])
            store.start()
            stores.append(store)
        for store in stores:
            store.wait()

    return pl.pallas_call(
        body,
        out_shape=jax.ShapeDtypeStruct((half, width), jnp.bfloat16),
        in_specs=[SMEM] + [VMEM] * 5,
        out_specs=HBM,
        scratch_shapes=[
            pltpu.VMEM((aux, width), jnp.bfloat16),
            pltpu.VMEM((half, width), jnp.bfloat16),
            pltpu.SemaphoreType.DMA((pieces,)),
        ],
        compiler_params=params(32),
        name="finish",
    )(in_smem(table), sums, other_sums, near, arrived, cycle_rows)


def shards(amp_tiles, tile_coords, tile_mask, pair_orbs, ladder_factor, cycle_factor):
    cores, pairs = lax.axis_size("virt"), lax.axis_size("pair")
    assert cores == 2 and pairs % 2 == 0
    own = amp_tiles[0]
    place = lax.axis_index("virt").astype(jnp.int32).reshape(1)
    swap = [(0, 1), (1, 0)]
    other = lax.ppermute(own, "virt", swap)
    square = pairs == 8
    table, own, cycle_rows, start = prepare(tile_coords[0].T, tile_mask, pair_orbs, place, own, cycle_factor)
    message, held = intermediate(table, own, other, cycle_rows, start, cores=cores)
    factor = ladder_factor[0]
    tile = held.shape[1]

    def exchange(value, first_core, second_core):
        partners = (first_core, second_core)
        routes = [(p * 2 + c, (p ^ partners[c]) * 2 + c) for p in range(pairs) for c in range(2)]
        return lax.ppermute(value, ("pair", "virt"), routes)

    if square:
        arrival = exchange(message, 4, 2)
        message, pair_orbs, held, factor = lax.optimization_barrier((message, pair_orbs, held, factor))
        next_orbs = lax.ppermute(pair_orbs, "pair", [(p, p ^ 1) for p in range(pairs)])
        left = ladder_build(table, held, factor)
        arrival, left = lax.optimization_barrier((arrival, left))
        kept, message = step(table, next_orbs, message, arrival, plain=0)
        message, left = lax.optimization_barrier((message, left))
        arrival = exchange(message, 2, 1)
        far = ladder_multiply(table, left, factor, tile, far=True, flops=10**10)
        arrival, far = lax.optimization_barrier((arrival, far))
        kept, message = step(table, next_orbs, kept, arrival, plain=1)
        message, left, far = lax.optimization_barrier((message, left, far))
        arrival = exchange(message, 1, 4)
        arrived = lax.ppermute(far, "virt", swap)
        near = ladder_multiply(table, left, factor, tile, far=False, flops=4 * 10**10)
        arrival, near = lax.optimization_barrier((arrival, near))
        sums = last_step(kept, arrival)
    else:
        left = ladder_build(table, held, factor)
        far = ladder_multiply(table, left, factor, tile, far=True, flops=10**10)
        near = ladder_multiply(table, left, factor, tile, far=False, flops=10**10)
        arrived = lax.ppermute(far, "virt", swap)
        width = factor.shape[0]
        right = pair_orbs[0, 1]
        occupied = jnp.arange(cycle_factor.shape[0], dtype=jnp.int32) == right
        mine = message[:, :width].astype(jnp.float32)
        total = lax.psum(jnp.where(occupied[:, None, None], mine[None], 0.0), "pair")
        sums = lax.dynamic_index_in_dim(total, right, 0, keepdims=False).astype(jnp.bfloat16)

    other_sums = lax.ppermute(sums, "virt", swap)
    return finish(table, sums, other_sums, near, arrived, cycle_rows, pieces=4)[None]


def solution(mesh):
    in_specs = (
        P(("groups", "pair"), "virt", None, None),
        P(("groups", "pair"), None, None),
        P(("groups", "pair"), None),
        P(("groups", "pair"), None),
        P(("groups", "virt"), None, None),
        P("groups", None, None),
    )
    out_specs = P(("groups", "pair"), "virt", None)
    return jax.shard_map(shards, mesh=mesh, in_specs=in_specs, out_specs=out_specs, check_vma=False)
```

```python
import functools

import jax
import jax.numpy as jnp
from jax import lax
from jax.experimental import pallas as pl
from jax.experimental.pallas import tpu as pltpu
from jax.sharding import PartitionSpec as P

LANES, LABEL = 128, 16
SMEM = pl.BlockSpec(memory_space=pltpu.SMEM)
VMEM = pl.BlockSpec(memory_space=pltpu.VMEM)
HBM = pl.BlockSpec(memory_space=pltpu.HBM)
FIRST_FIRST = (((0,), (0,)), ((), ()))
LAST_LAST = (((1,), (1,)), ((), ()))
COLUMN, ROW, KEPT, SORTED, NAME, BEGIN, FACTS = range(7)
USED, CORE, ORBITAL = range(3)


def params(mib):
    return pltpu.CompilerParams(vmem_limit_bytes=mib * 2**20)


def block(index, size):
    return pl.ds(pl.multiple_of(index * size, size), size)


def in_hbm(array):
    return pltpu.with_memory_space_constraint(array, pltpu.HBM)


def in_smem(array):
    return pltpu.with_memory_space_constraint(array, pltpu.SMEM)


def add_terms(total, table, rows, tiles, slots):
    size = tiles.shape[1]
    terms = [
        lax.dot_general(
            rows[block(table[COLUMN, s], size), :], tiles[k], FIRST_FIRST, preferred_element_type=jnp.float32
        )
        for k, s in enumerate(slots)
    ]
    for s, term in zip(slots, terms):
        total[:, block(table[ROW, s], size)] += term * table[KEPT, s].astype(jnp.float32)


def prepare(coords, mask, orbs, place, own, cycle_factor):
    slots = coords.shape[1]
    local, tile = own.shape[0], own.shape[1]
    width, aux = cycle_factor.shape[1:]
    tiles = width // tile
    places = max(slots + 1, tiles + 3)

    def body(coords, mask, orbs, place, own, factor, table, held, rows, total, s_coords, s_mask, s_orbs, count, sems):
        loads = [
            pltpu.make_async_copy(source, target, sems.at[n])
            for n, (source, target) in enumerate([(orbs, s_orbs), (coords, s_coords), (mask, s_mask), (own, held)])
        ]
        for load in loads:
            load.start()
        core = place[0]
        total[...] = jnp.zeros_like(total)
        loads[0].wait()
        load_rows = pltpu.make_async_copy(factor.at[s_orbs[0, 0]], rows, sems.at[4])
        load_rows.start()
        table[FACTS, CORE] = core
        table[FACTS, ORBITAL] = s_orbs[0, 1]

        for n in range(tiles):
            count[n] = 0
        loads[1].wait()
        loads[2].wait()
        for s in range(slots):
            g = lax.rem(s + core * local, slots)
            d, kept = s_coords[1, g], s_mask[0, g]
            table[COLUMN, s] = s_coords[0, g]
            table[ROW, s] = d
            table[KEPT, s] = kept
            table[SORTED, s] = slots
            count[d] += (kept != 0).astype(jnp.int32)
        table[COLUMN, slots] = 0
        begin, used = jnp.int32(0), jnp.int32(0)
        for n in range(tiles):
            here = count[n]
            table[NAME, used] = n
            table[BEGIN, used] = begin
            count[n] = begin
            begin += here
            used += (here > 0).astype(jnp.int32)
        table[FACTS, USED] = used
        for n in range(3):
            table[NAME, used + n] = 0
            table[BEGIN, used + n] = begin
        for s in range(slots):
            d = table[ROW, s]
            at = count[d]
            kept = table[KEPT, s] != 0
            table[SORTED, jnp.where(kept, at, slots)] = s
            count[d] = at + kept.astype(jnp.int32)
        loads[3].wait()
        load_rows.wait()
        add_terms(total, table, rows, held, range(local))

    return pl.pallas_call(
        body,
        out_shape=[
            pltpu.SMEM((7, places), jnp.int32),
            jax.ShapeDtypeStruct(own.shape, own.dtype),
            jax.ShapeDtypeStruct((width, aux), jnp.bfloat16),
            jax.ShapeDtypeStruct((aux, width), jnp.float32),
        ],
        in_specs=[HBM, HBM, HBM, SMEM, HBM, HBM],
        out_specs=[SMEM, VMEM, VMEM, VMEM],
        scratch_shapes=[
            pltpu.SMEM(coords.shape, jnp.int32),
            pltpu.SMEM(mask.shape, jnp.int32),
            pltpu.SMEM(orbs.shape, jnp.int32),
            pltpu.SMEM((tiles,), jnp.int32),
            pltpu.SemaphoreType.DMA((5,)),
        ],
        compiler_params=params(16),
        name="prepare",
    )(in_hbm(coords), in_hbm(mask), in_hbm(orbs), place, in_hbm(own), in_hbm(cycle_factor))


def intermediate(table, own, other, rows, start, *, cores):
    local, tile = own.shape[0], own.shape[1]
    aux, width = start.shape
    share = aux // cores

    def body(table, own, other, rows, start, out, held, total):
        total[...] = start[...]
        add_terms(total, table, rows, other, range(local, 2 * local))
        for n in range(width // LANES):
            out[n * share : (n + 1) * share, :] = total[
                block(table[FACTS, CORE], share), n * LANES : (n + 1) * LANES
            ].astype(out.dtype)
        label = jnp.zeros((LABEL, LANES), jnp.float32) + table[FACTS, ORBITAL].astype(jnp.float32)
        out[share * width // LANES :, :] = label.astype(out.dtype)
        held[:local] = own[...]
        held[local : 2 * local] = other[...]
        held[2 * local] = jnp.zeros((tile, tile), held.dtype)

    return pl.pallas_call(
        body,
        out_shape=[
            jax.ShapeDtypeStruct((share * width // LANES + LABEL, LANES), jnp.bfloat16),
            jax.ShapeDtypeStruct((2 * local + 1, tile, tile), jnp.bfloat16),
        ],
        in_specs=[SMEM, VMEM, VMEM, VMEM, VMEM],
        out_specs=[VMEM, VMEM],
        scratch_shapes=[pltpu.VMEM((aux, width), jnp.float32)],
        compiler_params=params(16),
        name="intermediate",
    )(in_smem(table), own, other, rows, start)


def step(table, next_orbs, mine, arrival, *, plain):
    length = arrival.shape[0] - LABEL

    def body(table, next_orbs, mine, arrival, kept, out):
        value = mine[:length, :].astype(jnp.float32)
        extra = arrival[:length, :].astype(jnp.float32)
        own = jnp.zeros((LABEL, LANES), jnp.float32) + table[FACTS, ORBITAL].astype(jnp.float32)
        out[length:, :] = own.astype(out.dtype)

        @pl.when(table[FACTS, CORE] == plain)
        def _():
            total = value + extra
            kept[...] = total
            out[:length, :] = total.astype(out.dtype)

        @pl.when(table[FACTS, CORE] != plain)
        def _():
            label = own[:1, :]
            theirs = arrival[length : length + LABEL, :].astype(jnp.float32)[:1, :]
            behind = next_orbs[0:1, 1:2].astype(jnp.float32)
            kept[...] = value + jnp.where(theirs == label, extra, 0.0)
            out[:length, :] = (
                jnp.where(label == behind, value, 0.0) + jnp.where(theirs == behind, extra, 0.0)
            ).astype(out.dtype)

    return pl.pallas_call(
        body,
        out_shape=[
            jax.ShapeDtypeStruct((length, LANES), jnp.float32),
            jax.ShapeDtypeStruct(arrival.shape, arrival.dtype),
        ],
        in_specs=[SMEM, VMEM, VMEM, VMEM],
        out_specs=[VMEM, VMEM],
        compiler_params=params(16),
        name="step",
    )(in_smem(table), next_orbs, mine, arrival)


def last_step(mine, arrival):
    length = mine.shape[0]

    def body(mine, arrival, out):
        out[...] = (mine[...] + arrival[:length, :].astype(jnp.float32)).astype(out.dtype)

    return pl.pallas_call(
        body,
        out_shape=jax.ShapeDtypeStruct(mine.shape, arrival.dtype),
        in_specs=[VMEM, VMEM],
        out_specs=VMEM,
        compiler_params=params(16),
        name="last_step",
    )(mine, arrival)


def ladder_build(table, held, factor):
    empty, tile = held.shape[0] - 1, held.shape[1]
    width = factor.shape[0]
    pairs = -(-(width // tile) // 2)

    def body(table, held, factor, left, wide):
        def two_tiles(m, carry):
            first, second, end = [table[BEGIN, 2 * m + k] for k in range(3)]
            here = block(m, 2 * tile)

            def product(at, count):
                columns, weights = [], []
                for k in range(count):
                    s = jnp.where(at + k < end, table[SORTED, jnp.minimum(at + k, empty)], empty)
                    columns.append(factor[:, block(table[COLUMN, s], tile)])
                    value, none = held[s], jnp.zeros((tile, tile), held.dtype)
                    early = at + k < second
                    weights.append(
                        jnp.concatenate([jnp.where(early, value, none), jnp.where(early, none, value)], axis=1)
                    )
                return jnp.dot(
                    jnp.concatenate(columns, axis=1), jnp.concatenate(weights, axis=0),
                    preferred_element_type=jnp.float32,
                )

            rounds = (end - first + 1) // 2
            for n in range(1, 4):

                @pl.when(rounds == n)
                def _():
                    left[:, here] = product(first, 2 * n).astype(left.dtype)

            @pl.when(rounds > 3)
            def _():
                wide[...] = product(first, 2)

                def add(t, carry):
                    wide[...] += product(first + 2 * t, 2)
                    return carry

                lax.fori_loop(1, rounds, add, 0)
                left[:, here] = wide[...].astype(left.dtype)

            return carry

        lax.fori_loop(0, (table[FACTS, USED] + 1) // 2, two_tiles, 0)

    wide = pltpu.VMEM((width, 2 * tile), jnp.float32)
    return ladder_call(body, [(width, 2 * pairs * tile)], [wide], in_smem(table), held, factor, flops=10**10)[0]


def early_unit(core, steps):
    return jnp.logical_and(core == 1, steps <= 4)


def ladder_multiply(table, left, factor, tile, outputs, *, flops):
    half = left.shape[0] // 2

    def body(table, left, factor, *outs):
        core = table[FACTS, CORE]
        steps = (table[FACTS, USED] + 1) // 2
        for n in range(factor.shape[0] // tile // 2 + 1):

            @pl.when(steps == n)
            def _():
                for (far, first, end, when), out in zip(outputs, outs):
                    rows = block(1 - core if far else core, half)
                    last = end
                    if when is not None:
                        chosen = early_unit(core, n) if when == "early" else jnp.logical_not(early_unit(core, n))
                        last = jnp.where(chosen, end, first)

                    def unit(k, carry):
                        if n == 0:
                            out[k - first] = jnp.zeros((half, half), out.dtype)
                            return carry
                        here = block(k, half)
                        right = jnp.concatenate(
                            [factor[here, block(table[NAME, w], tile)] for w in range(2 * n)], axis=1
                        )
                        out[k - first] = lax.dot_general(
                            left[rows, : 2 * n * tile], right, LAST_LAST, preferred_element_type=jnp.float32
                        ).astype(out.dtype)
                        return carry

                    lax.fori_loop(first, last, unit, 0)

    shapes = [(end - first, half, half) for far, first, end, when in outputs]
    return ladder_call(body, shapes, [], in_smem(table), left, factor, flops=flops)


def ladder_call(body, shapes, scratch, *operands, flops):
    return pl.pallas_call(
        body,
        out_shape=[jax.ShapeDtypeStruct(shape, jnp.bfloat16) for shape in shapes],
        in_specs=[SMEM] + [VMEM] * (len(operands) - 1),
        out_specs=[VMEM] * len(shapes),
        scratch_shapes=scratch,
        compiler_params=params(32),
        cost_estimate=pl.CostEstimate(flops=flops, bytes_accessed=1, transcendentals=0),
        name="ladder",
    )(*operands)


def lay_out(sums, low, core):
    share = low.shape[0] // 2
    for n in range(low.shape[1] // LANES):
        side = slice(n * LANES, (n + 1) * LANES)
        low[block(core, share), side] = sums[n * share : (n + 1) * share, :]
        low[block(1 - core, share), side] = jnp.zeros((share, LANES), low.dtype)


def first_terms(table, sums, near, arrived, cycle_rows, *, pieces):
    half, width = arrived.shape[1], 2 * arrived.shape[2]
    aux = cycle_rows.shape[1]
    rows = half // pieces

    def body(table, sums, near_early, near_late, near_b, arrived, factor, out, low):
        core = table[FACTS, CORE]
        early = early_unit(core, (table[FACTS, USED] + 1) // 2)
        lay_out(sums, low, core)
        for n in range(pieces):
            here = slice(n * rows, (n + 1) * rows)
            term = jnp.dot(
                factor[pl.ds(pl.multiple_of(core * half + n * rows, rows), rows), :], low[...],
                preferred_element_type=jnp.float32,
            )
            near_a = jnp.where(early, near_early[0, here, :], near_late[0, here, :])
            for k, near in enumerate([near_a, near_b[0, here, :]]):
                side = slice(k * half, (k + 1) * half)
                ladder = near.astype(jnp.float32) + arrived[k, here, :].astype(jnp.float32)
                out[here, side] = ladder + term[:, side]

    return pl.pallas_call(
        body,
        out_shape=jax.ShapeDtypeStruct((half, width), jnp.float32),
        in_specs=[SMEM] + [VMEM] * 6,
        out_specs=VMEM,
        scratch_shapes=[pltpu.VMEM((aux, width), jnp.bfloat16)],
        compiler_params=params(32),
        cost_estimate=pl.CostEstimate(flops=10**9, bytes_accessed=1, transcendentals=0),
        name="first_terms",
    )(in_smem(table), sums, *near, arrived, cycle_rows)


def finish(table, other_sums, terms, cycle_rows, *, pieces):
    half, width = terms.shape
    aux = cycle_rows.shape[1]
    rows = half // pieces

    def body(table, other_sums, terms, factor, out, low, done, sems):
        core = table[FACTS, CORE]
        lay_out(other_sums, low, 1 - core)
        stores = []
        for n in range(pieces):
            here = slice(n * rows, (n + 1) * rows)
            term = jnp.dot(
                factor[pl.ds(pl.multiple_of(core * half + n * rows, rows), rows), :], low[...],
                preferred_element_type=jnp.float32,
            )
            done[here, :] = (terms[here, :] + term).astype(done.dtype)
            store = pltpu.make_async_copy(done.at[here, :], out.at[here, :], sems.at[n])
            store.start()
            stores.append(store)
        for store in stores:
            store.wait()

    return pl.pallas_call(
        body,
        out_shape=jax.ShapeDtypeStruct((half, width), jnp.bfloat16),
        in_specs=[SMEM] + [VMEM] * 3,
        out_specs=HBM,
        scratch_shapes=[
            pltpu.VMEM((aux, width), jnp.bfloat16),
            pltpu.VMEM((half, width), jnp.bfloat16),
            pltpu.SemaphoreType.DMA((pieces,)),
        ],
        compiler_params=params(32),
        name="finish",
    )(in_smem(table), other_sums, terms, cycle_rows)


def shards(amp_tiles, tile_coords, tile_mask, pair_orbs, ladder_factor, cycle_factor):
    cores, pairs = lax.axis_size("virt"), lax.axis_size("pair")
    assert cores == 2 and pairs % 2 == 0
    own = amp_tiles[0]
    place = lax.axis_index("virt").astype(jnp.int32).reshape(1)
    swap = [(0, 1), (1, 0)]
    other = lax.ppermute(own, "virt", swap)
    square = pairs == 8
    table, own, cycle_rows, start = prepare(tile_coords[0].T, tile_mask, pair_orbs, place, own, cycle_factor)
    message, held = intermediate(table, own, other, cycle_rows, start, cores=cores)
    factor = ladder_factor[0]
    tile = held.shape[1]

    def exchange(value, first_core, second_core):
        partners = (first_core, second_core)
        routes = [(p * 2 + c, (p ^ partners[c]) * 2 + c) for p in range(pairs) for c in range(2)]
        return lax.ppermute(value, ("pair", "virt"), routes)

    if square:
        arrival = exchange(message, 4, 2)
        message, pair_orbs, held, factor = lax.optimization_barrier((message, pair_orbs, held, factor))
        next_orbs = lax.ppermute(pair_orbs, "pair", [(p, p ^ 1) for p in range(pairs)])
        left = ladder_build(table, held, factor)
        arrival, left = lax.optimization_barrier((arrival, left))
        kept, message = step(table, next_orbs, message, arrival, plain=0)
        message, left = lax.optimization_barrier((message, left))
        arrival = exchange(message, 2, 1)
        far, near_early = ladder_multiply(
            table, left, factor, tile, [(True, 0, 2, None), (False, 0, 1, "early")], flops=10**10
        )
        arrival, far = lax.optimization_barrier((arrival, far))
        kept, message = step(table, next_orbs, kept, arrival, plain=1)
        message, left, far = lax.optimization_barrier((message, left, far))
        arrival = exchange(message, 1, 4)
        arrived = lax.ppermute(far, "virt", swap)
        near_late, near_b = ladder_multiply(
            table, left, factor, tile, [(False, 0, 1, "late"), (False, 1, 2, None)], flops=4 * 10**10
        )
        arrival, near_b = lax.optimization_barrier((arrival, near_b))
        sums = last_step(kept, arrival)
    else:
        left = ladder_build(table, held, factor)
        far, near_early = ladder_multiply(
            table, left, factor, tile, [(True, 0, 2, None), (False, 0, 1, "early")], flops=10**10
        )
        near_late, near_b = ladder_multiply(
            table, left, factor, tile, [(False, 0, 1, "late"), (False, 1, 2, None)], flops=10**10
        )
        arrived = lax.ppermute(far, "virt", swap)
        right = pair_orbs[0, 1]
        occupied = jnp.arange(cycle_factor.shape[0], dtype=jnp.int32) == right
        mine = message[:-LABEL].astype(jnp.float32)
        total = lax.psum(jnp.where(occupied[:, None, None], mine[None], 0.0), "pair")
        sums = lax.dynamic_index_in_dim(total, right, 0, keepdims=False).astype(jnp.bfloat16)

    other_sums = lax.ppermute(sums, "virt", swap)
    terms = first_terms(table, sums, [near_early, near_late, near_b], arrived, cycle_rows, pieces=4)
    return finish(table, other_sums, terms, cycle_rows, pieces=6)[None]


def solution(mesh):
    in_specs = (
        P(("groups", "pair"), "virt", None, None),
        P(("groups", "pair"), None, None),
        P(("groups", "pair"), None),
        P(("groups", "pair"), None),
        P(("groups", "virt"), None, None),
        P("groups", None, None),
    )
    out_specs = P(("groups", "pair"), "virt", None)
    return jax.shard_map(shards, mesh=mesh, in_specs=in_specs, out_specs=out_specs, check_vma=False)
```

```python
import functools

import jax
import jax.numpy as jnp
from jax import lax
from jax.experimental import pallas as pl
from jax.experimental.pallas import tpu as pltpu
from jax.sharding import PartitionSpec as P

LANES, LABEL = 128, 16
ORDERS = (4, 2, 1), (2, 1, 4)
SMEM = pl.BlockSpec(memory_space=pltpu.SMEM)
VMEM = pl.BlockSpec(memory_space=pltpu.VMEM)
HBM = pl.BlockSpec(memory_space=pltpu.HBM)
FIRST_FIRST = (((0,), (0,)), ((), ()))
LAST_LAST = (((1,), (1,)), ((), ()))
COLUMN, ROW, KEPT, SORTED, NAME, BEGIN, FACTS = range(7)
USED, CORE, ORBITAL = range(3)


def params(mib):
    return pltpu.CompilerParams(vmem_limit_bytes=mib * 2**20)


def block(index, size):
    return pl.ds(pl.multiple_of(index * size, size), size)


def in_hbm(array):
    return pltpu.with_memory_space_constraint(array, pltpu.HBM)


def in_smem(array):
    return pltpu.with_memory_space_constraint(array, pltpu.SMEM)


def add_terms(total, table, rows, tiles, slots):
    size = tiles.shape[1]
    terms = [
        lax.dot_general(
            rows[block(table[COLUMN, s], size), :], tiles[k], FIRST_FIRST, preferred_element_type=jnp.float32
        )
        for k, s in enumerate(slots)
    ]
    for s, term in zip(slots, terms):
        total[:, block(table[ROW, s], size)] += term * table[KEPT, s].astype(jnp.float32)


def prepare(coords, mask, orbs, place, own, cycle_factor):
    slots = coords.shape[1]
    local, tile = own.shape[0], own.shape[1]
    width, aux = cycle_factor.shape[1:]
    tiles = width // tile
    places = max(slots + 1, tiles + 3)

    def body(coords, mask, orbs, place, own, factor, table, held, rows, total, s_coords, s_mask, s_orbs, count, sems):
        loads = [
            pltpu.make_async_copy(source, target, sems.at[n])
            for n, (source, target) in enumerate([(orbs, s_orbs), (coords, s_coords), (mask, s_mask), (own, held)])
        ]
        for load in loads:
            load.start()
        core = place[0]
        total[...] = jnp.zeros_like(total)
        loads[0].wait()
        load_rows = pltpu.make_async_copy(factor.at[s_orbs[0, 0]], rows, sems.at[4])
        load_rows.start()
        table[FACTS, CORE] = core
        table[FACTS, ORBITAL] = s_orbs[0, 1]

        for n in range(tiles):
            count[n] = 0
        loads[1].wait()
        loads[2].wait()
        for s in range(slots):
            g = lax.rem(s + core * local, slots)
            d, kept = s_coords[1, g], s_mask[0, g]
            table[COLUMN, s] = s_coords[0, g]
            table[ROW, s] = d
            table[KEPT, s] = kept
            table[SORTED, s] = slots
            count[d] += (kept != 0).astype(jnp.int32)
        table[COLUMN, slots] = 0
        begin, used = jnp.int32(0), jnp.int32(0)
        for n in range(tiles):
            here = count[n]
            table[NAME, used] = n
            table[BEGIN, used] = begin
            count[n] = begin
            begin += here
            used += (here > 0).astype(jnp.int32)
        table[FACTS, USED] = used
        for n in range(3):
            table[NAME, used + n] = 0
            table[BEGIN, used + n] = begin
        for s in range(slots):
            d = table[ROW, s]
            at = count[d]
            kept = table[KEPT, s] != 0
            table[SORTED, jnp.where(kept, at, slots)] = s
            count[d] = at + kept.astype(jnp.int32)
        loads[3].wait()
        load_rows.wait()
        add_terms(total, table, rows, held, range(local))

    return pl.pallas_call(
        body,
        out_shape=[
            pltpu.SMEM((7, places), jnp.int32),
            jax.ShapeDtypeStruct(own.shape, own.dtype),
            jax.ShapeDtypeStruct((width, aux), jnp.bfloat16),
            jax.ShapeDtypeStruct((aux, width), jnp.float32),
        ],
        in_specs=[HBM, HBM, HBM, SMEM, HBM, HBM],
        out_specs=[SMEM, VMEM, VMEM, VMEM],
        scratch_shapes=[
            pltpu.SMEM(coords.shape, jnp.int32),
            pltpu.SMEM(mask.shape, jnp.int32),
            pltpu.SMEM(orbs.shape, jnp.int32),
            pltpu.SMEM((tiles,), jnp.int32),
            pltpu.SemaphoreType.DMA((5,)),
        ],
        compiler_params=params(16),
        name="prepare",
    )(in_hbm(coords), in_hbm(mask), in_hbm(orbs), place, in_hbm(own), in_hbm(cycle_factor))


def intermediate(table, own, other, rows, start, *, cores):
    local, tile = own.shape[0], own.shape[1]
    aux, width = start.shape
    blocks = width // LANES // cores

    def body(table, own, other, rows, start, out, held, total):
        total[...] = start[...]
        add_terms(total, table, rows, other, range(local, 2 * local))
        for n in range(blocks):
            out[n * aux : (n + 1) * aux, :] = total[
                :, block(table[FACTS, CORE] * blocks + n, LANES)
            ].astype(out.dtype)
        label = jnp.zeros((LABEL, LANES), jnp.float32) + table[FACTS, ORBITAL].astype(jnp.float32)
        out[blocks * aux :, :] = label.astype(out.dtype)
        held[:local] = own[...]
        held[local : 2 * local] = other[...]
        held[2 * local] = jnp.zeros((tile, tile), held.dtype)

    return pl.pallas_call(
        body,
        out_shape=[
            jax.ShapeDtypeStruct((blocks * aux + LABEL, LANES), jnp.bfloat16),
            jax.ShapeDtypeStruct((2 * local + 1, tile, tile), jnp.bfloat16),
        ],
        in_specs=[SMEM, VMEM, VMEM, VMEM, VMEM],
        out_specs=[VMEM, VMEM],
        scratch_shapes=[pltpu.VMEM((aux, width), jnp.float32)],
        compiler_params=params(16),
        name="intermediate",
    )(in_smem(table), own, other, rows, start)


def step(table, next_orbs, mine, arrival, *, plain):
    length = arrival.shape[0] - LABEL

    def body(table, next_orbs, mine, arrival, kept, out):
        value = mine[:length, :].astype(jnp.float32)
        extra = arrival[:length, :].astype(jnp.float32)
        own = jnp.zeros((LABEL, LANES), jnp.float32) + table[FACTS, ORBITAL].astype(jnp.float32)
        out[length:, :] = own.astype(out.dtype)

        @pl.when(table[FACTS, CORE] == plain)
        def _():
            total = value + extra
            kept[...] = total
            out[:length, :] = total.astype(out.dtype)

        @pl.when(table[FACTS, CORE] != plain)
        def _():
            label = own[:1, :]
            theirs = arrival[length : length + LABEL, :].astype(jnp.float32)[:1, :]
            behind = next_orbs[0:1, 1:2].astype(jnp.float32)
            kept[...] = value + jnp.where(theirs == label, extra, 0.0)
            out[:length, :] = (
                jnp.where(label == behind, value, 0.0) + jnp.where(theirs == behind, extra, 0.0)
            ).astype(out.dtype)

    return pl.pallas_call(
        body,
        out_shape=[
            jax.ShapeDtypeStruct((length, LANES), jnp.float32),
            jax.ShapeDtypeStruct(arrival.shape, arrival.dtype),
        ],
        in_specs=[SMEM, VMEM, VMEM, VMEM],
        out_specs=[VMEM, VMEM],
        compiler_params=params(16),
        name="step",
    )(in_smem(table), next_orbs, mine, arrival)


def last_step(mine, arrival):
    length = mine.shape[0]

    def body(mine, arrival, out):
        out[...] = (mine[...] + arrival[:length, :].astype(jnp.float32)).astype(out.dtype)

    return pl.pallas_call(
        body,
        out_shape=jax.ShapeDtypeStruct(mine.shape, arrival.dtype),
        in_specs=[VMEM, VMEM],
        out_specs=VMEM,
        compiler_params=params(16),
        name="last_step",
    )(mine, arrival)


def ladder_build(table, held, factor):
    empty, tile = held.shape[0] - 1, held.shape[1]
    width = factor.shape[0]
    pairs = -(-(width // tile) // 2)

    def body(table, held, factor, left, wide):
        def two_tiles(m, carry):
            first, second, end = [table[BEGIN, 2 * m + k] for k in range(3)]
            here = block(m, 2 * tile)

            def product(at, count):
                columns, weights = [], []
                for k in range(count):
                    s = jnp.where(at + k < end, table[SORTED, jnp.minimum(at + k, empty)], empty)
                    columns.append(factor[:, block(table[COLUMN, s], tile)])
                    value, none = held[s], jnp.zeros((tile, tile), held.dtype)
                    early = at + k < second
                    weights.append(
                        jnp.concatenate([jnp.where(early, value, none), jnp.where(early, none, value)], axis=1)
                    )
                return jnp.dot(
                    jnp.concatenate(columns, axis=1), jnp.concatenate(weights, axis=0),
                    preferred_element_type=jnp.float32,
                )

            rounds = (end - first + 1) // 2
            for n in range(1, 4):

                @pl.when(rounds == n)
                def _():
                    left[:, here] = product(first, 2 * n).astype(left.dtype)

            @pl.when(rounds > 3)
            def _():
                wide[...] = product(first, 2)

                def add(t, carry):
                    wide[...] += product(first + 2 * t, 2)
                    return carry

                lax.fori_loop(1, rounds, add, 0)
                left[:, here] = wide[...].astype(left.dtype)

            return carry

        lax.fori_loop(0, (table[FACTS, USED] + 1) // 2, two_tiles, 0)

    wide = pltpu.VMEM((width, 2 * tile), jnp.float32)
    return ladder_call(body, (width, 2 * pairs * tile), [wide], in_smem(table), held, factor, flops=10**10)


def ladder_multiply(table, left, factor, tile, *, far, flops):
    half = left.shape[0] // 2

    def body(table, left, factor, out):
        core = table[FACTS, CORE]
        rows = block(1 - core if far else core, half)
        steps = (table[FACTS, USED] + 1) // 2
        for n in range(factor.shape[0] // tile // 2 + 1):

            @pl.when(steps == n)
            def _():
                def unit(k, carry):
                    if n == 0:
                        out[k] = jnp.zeros((half, half), out.dtype)
                        return carry
                    here = block(k, half)
                    right = jnp.concatenate(
                        [factor[here, block(table[NAME, w], tile)] for w in range(2 * n)], axis=1
                    )
                    out[k] = lax.dot_general(
                        left[rows, : 2 * n * tile], right, LAST_LAST, preferred_element_type=jnp.float32
                    ).astype(out.dtype)
                    return carry

                lax.fori_loop(0, 2, unit, 0)

    return ladder_call(body, (2, half, half), [], in_smem(table), left, factor, flops=flops)


def ladder_call(body, shape, scratch, *operands, flops):
    return pl.pallas_call(
        body,
        out_shape=jax.ShapeDtypeStruct(shape, jnp.bfloat16),
        in_specs=[SMEM] + [VMEM] * (len(operands) - 1),
        out_specs=VMEM,
        scratch_shapes=scratch,
        compiler_params=params(32),
        cost_estimate=pl.CostEstimate(flops=flops, bytes_accessed=1, transcendentals=0),
        name="ladder",
    )(*operands)


def finish(table, sums, near, arrived, cycle_rows, whole, *, pieces):
    half = arrived.shape[1]
    aux = cycle_rows.shape[1]
    rows = half // pieces
    first = whole is None

    def body(table, sums, near, arrived, factor, *refs):
        out, low, done, sems = refs[-4:]
        core = table[FACTS, CORE]
        side = core if first else 1 - core
        for n in range(half // LANES):
            low[:, n * LANES : (n + 1) * LANES] = sums[n * aux : (n + 1) * aux, :]
        stores = []
        for n in range(pieces):
            here = slice(n * rows, (n + 1) * rows)
            term = jnp.dot(
                factor[pl.ds(pl.multiple_of(core * half + n * rows, rows), rows), :], low[...],
                preferred_element_type=jnp.float32,
            )
            ladder = near[side, here, :].astype(jnp.float32) + arrived[side, here, :].astype(jnp.float32)
            total = ladder + term
            done[here, :] = total.astype(done.dtype)
            store = pltpu.make_async_copy(
                done.at[here, :], out.at[here, block(side, half)], sems.at[n]
            )
            store.start()
            stores.append(store)
        for store in stores:
            store.wait()

    operands = [in_smem(table), sums, near, arrived, cycle_rows]
    return pl.pallas_call(
        body,
        out_shape=jax.ShapeDtypeStruct((half, 2 * half), jnp.bfloat16),
        in_specs=[SMEM] + [VMEM] * 4 + [HBM] * (not first),
        out_specs=HBM,
        scratch_shapes=[
            pltpu.VMEM((aux, half), jnp.bfloat16),
            pltpu.VMEM((half, half), jnp.bfloat16),
            pltpu.SemaphoreType.DMA((pieces,)),
        ],
        input_output_aliases={} if first else {len(operands): 0},
        compiler_params=params(16),
        cost_estimate=pl.CostEstimate(flops=10**9, bytes_accessed=1, transcendentals=0),
        name="finish_own" if first else "finish_other",
    )(*operands, *([] if first else [whole]))


def shards(amp_tiles, tile_coords, tile_mask, pair_orbs, ladder_factor, cycle_factor):
    cores, pairs = lax.axis_size("virt"), lax.axis_size("pair")
    assert cores == 2 and pairs % 2 == 0
    own = amp_tiles[0]
    place = lax.axis_index("virt").astype(jnp.int32).reshape(1)
    swap = [(0, 1), (1, 0)]
    other = lax.ppermute(own, "virt", swap)
    square = pairs == 8
    table, own, cycle_rows, start = prepare(tile_coords[0].T, tile_mask, pair_orbs, place, own, cycle_factor)
    message, held = intermediate(table, own, other, cycle_rows, start, cores=cores)
    factor = ladder_factor[0]
    tile = held.shape[1]

    def exchange(value, *partners):
        routes = [(p * 2 + c, (p ^ partners[c]) * 2 + c) for p in range(pairs) for c in range(2)]
        return lax.ppermute(value, ("pair", "virt"), routes)

    if square:
        arrival = exchange(message, ORDERS[0][0], ORDERS[1][0])
        message, pair_orbs, held, factor = lax.optimization_barrier((message, pair_orbs, held, factor))
        next_orbs = exchange(pair_orbs, ORDERS[0][2], ORDERS[1][1])
        left = ladder_build(table, held, factor)
        arrival, left = lax.optimization_barrier((arrival, left))
        kept, message = step(table, next_orbs, message, arrival, plain=0)
        message, left = lax.optimization_barrier((message, left))
        arrival = exchange(message, ORDERS[0][1], ORDERS[1][1])
        far = ladder_multiply(table, left, factor, tile, far=True, flops=10**10)
        arrival, far = lax.optimization_barrier((arrival, far))
        kept, message = step(table, next_orbs, kept, arrival, plain=1)
        message, left, far = lax.optimization_barrier((message, left, far))
        arrival = exchange(message, ORDERS[0][2], ORDERS[1][2])
        arrived = lax.ppermute(far, "virt", swap)
        near = ladder_multiply(table, left, factor, tile, far=False, flops=4 * 10**10)
        arrival, near = lax.optimization_barrier((arrival, near))
        sums = last_step(kept, arrival)
    else:
        left = ladder_build(table, held, factor)
        far = ladder_multiply(table, left, factor, tile, far=True, flops=10**10)
        near = ladder_multiply(table, left, factor, tile, far=False, flops=10**10)
        arrived = lax.ppermute(far, "virt", swap)
        right = pair_orbs[0, 1]
        occupied = jnp.arange(cycle_factor.shape[0], dtype=jnp.int32) == right
        mine = message[:-LABEL].astype(jnp.float32)
        total = lax.psum(jnp.where(occupied[:, None, None], mine[None], 0.0), "pair")
        sums = lax.dynamic_index_in_dim(total, right, 0, keepdims=False).astype(jnp.bfloat16)

    other_sums = lax.ppermute(sums, "virt", swap)
    own_side = finish(table, sums, near, arrived, cycle_rows, None, pieces=4)
    return finish(table, other_sums, near, arrived, cycle_rows, own_side, pieces=4)[None]


def solution(mesh):
    in_specs = (
        P(("groups", "pair"), "virt", None, None),
        P(("groups", "pair"), None, None),
        P(("groups", "pair"), None),
        P(("groups", "pair"), None),
        P(("groups", "virt"), None, None),
        P("groups", None, None),
    )
    out_specs = P(("groups", "pair"), "virt", None)
    return jax.shard_map(shards, mesh=mesh, in_specs=in_specs, out_specs=out_specs, check_vma=False)
```

```python
import functools

import jax
import jax.numpy as jnp
from jax import lax
from jax.experimental import pallas as pl
from jax.experimental.pallas import tpu as pltpu
from jax.sharding import PartitionSpec as P

LANES, LABEL = 128, 16
ORDERS = (4, 2, 1), (2, 1, 4)
SMEM = pl.BlockSpec(memory_space=pltpu.SMEM)
VMEM = pl.BlockSpec(memory_space=pltpu.VMEM)
HBM = pl.BlockSpec(memory_space=pltpu.HBM)
FIRST_FIRST = (((0,), (0,)), ((), ()))
LAST_LAST = (((1,), (1,)), ((), ()))
COLUMN, ROW, KEPT, SORTED, NAME, BEGIN, FACTS = range(7)
USED, CORE, ORBITAL = range(3)


def params(mib):
    return pltpu.CompilerParams(vmem_limit_bytes=mib * 2**20)


def block(index, size):
    return pl.ds(pl.multiple_of(index * size, size), size)


def in_hbm(array):
    return pltpu.with_memory_space_constraint(array, pltpu.HBM)


def in_smem(array):
    return pltpu.with_memory_space_constraint(array, pltpu.SMEM)


def add_terms(total, table, rows, tiles, slots):
    size = tiles.shape[1]
    terms = [
        lax.dot_general(
            rows[block(table[COLUMN, s], size), :], tiles[k], FIRST_FIRST, preferred_element_type=jnp.float32
        )
        for k, s in enumerate(slots)
    ]
    for s, term in zip(slots, terms):
        total[:, block(table[ROW, s], size)] += term * table[KEPT, s].astype(jnp.float32)


def prepare(coords, mask, orbs, place, own, cycle_factor, *, cores):
    slots = coords.shape[1]
    local, tile = own.shape[0], own.shape[1]
    width, aux = cycle_factor.shape[1:]
    tiles, tiles_here = width // tile, width // tile // cores
    places = max(slots + 1, tiles + 3)

    def body(coords, mask, orbs, place, own, factor, table, held, rows, total, s_coords, s_mask, s_orbs, count, sems):
        loads = [
            pltpu.make_async_copy(source, target, sems.at[n])
            for n, (source, target) in enumerate([(orbs, s_orbs), (coords, s_coords), (mask, s_mask), (own, held)])
        ]
        for load in loads:
            load.start()
        core = place[0]
        total[...] = jnp.zeros_like(total)
        loads[0].wait()
        load_rows = pltpu.make_async_copy(factor.at[s_orbs[0, 0]], rows, sems.at[4])
        load_rows.start()
        table[FACTS, CORE] = core
        table[FACTS, ORBITAL] = s_orbs[0, 1]

        for n in range(tiles):
            count[n] = 0
        loads[1].wait()
        loads[2].wait()
        for s in range(slots):
            g = lax.rem(s + core * local, slots)
            d, kept = s_coords[1, g], s_mask[0, g]
            table[COLUMN, s] = s_coords[0, g]
            inside = d // tiles_here == core
            table[ROW, s] = jnp.where(inside, d - core * tiles_here, 0)
            table[KEPT, s] = jnp.where(inside, kept, 0)
            table[SORTED, s] = slots
            count[d] += (kept != 0).astype(jnp.int32)
        table[COLUMN, slots] = 0
        begin, used = jnp.int32(0), jnp.int32(0)
        for n in range(tiles):
            here = count[n]
            table[NAME, used] = n
            table[BEGIN, used] = begin
            count[n] = begin
            begin += here
            used += (here > 0).astype(jnp.int32)
        table[FACTS, USED] = used
        for n in range(3):
            table[NAME, used + n] = 0
            table[BEGIN, used + n] = begin
        for s in range(slots):
            g = lax.rem(s + core * local, slots)
            d, kept = s_coords[1, g], s_mask[0, g] != 0
            at = count[d]
            table[SORTED, jnp.where(kept, at, slots)] = s
            count[d] = at + kept.astype(jnp.int32)
        loads[3].wait()
        load_rows.wait()
        add_terms(total, table, rows, held, range(local))

    return pl.pallas_call(
        body,
        out_shape=[
            pltpu.SMEM((7, places), jnp.int32),
            jax.ShapeDtypeStruct(own.shape, own.dtype),
            jax.ShapeDtypeStruct((width, aux), jnp.bfloat16),
            jax.ShapeDtypeStruct((aux, width // cores), jnp.float32),
        ],
        in_specs=[HBM, HBM, HBM, SMEM, HBM, HBM],
        out_specs=[SMEM, VMEM, VMEM, VMEM],
        scratch_shapes=[
            pltpu.SMEM(coords.shape, jnp.int32),
            pltpu.SMEM(mask.shape, jnp.int32),
            pltpu.SMEM(orbs.shape, jnp.int32),
            pltpu.SMEM((tiles,), jnp.int32),
            pltpu.SemaphoreType.DMA((5,)),
        ],
        compiler_params=params(16),
        name="prepare",
    )(in_hbm(coords), in_hbm(mask), in_hbm(orbs), place, in_hbm(own), in_hbm(cycle_factor))


def intermediate(table, own, other, rows, start):
    local, tile = own.shape[0], own.shape[1]
    aux, width = start.shape
    blocks = width // LANES

    def body(table, own, other, rows, start, out, held, total):
        total[...] = start[...]
        add_terms(total, table, rows, other, range(local, 2 * local))
        for n in range(blocks):
            out[n * aux : (n + 1) * aux, :] = total[:, n * LANES : (n + 1) * LANES].astype(out.dtype)
        label = jnp.zeros((LABEL, LANES), jnp.float32) + table[FACTS, ORBITAL].astype(jnp.float32)
        out[blocks * aux :, :] = label.astype(out.dtype)
        held[:local] = own[...]
        held[local : 2 * local] = other[...]
        held[2 * local] = jnp.zeros((tile, tile), held.dtype)

    return pl.pallas_call(
        body,
        out_shape=[
            jax.ShapeDtypeStruct((blocks * aux + LABEL, LANES), jnp.bfloat16),
            jax.ShapeDtypeStruct((2 * local + 1, tile, tile), jnp.bfloat16),
        ],
        in_specs=[SMEM, VMEM, VMEM, VMEM, VMEM],
        out_specs=[VMEM, VMEM],
        scratch_shapes=[pltpu.VMEM((aux, width), jnp.float32)],
        compiler_params=params(16),
        name="intermediate",
    )(in_smem(table), own, other, rows, start)


def step(table, next_orbs, mine, arrival, *, plain):
    length = arrival.shape[0] - LABEL

    def body(table, next_orbs, mine, arrival, kept, out):
        value = mine[:length, :].astype(jnp.float32)
        extra = arrival[:length, :].astype(jnp.float32)
        own = jnp.zeros((LABEL, LANES), jnp.float32) + table[FACTS, ORBITAL].astype(jnp.float32)
        out[length:, :] = own.astype(out.dtype)

        @pl.when(table[FACTS, CORE] == plain)
        def _():
            total = value + extra
            kept[...] = total
            out[:length, :] = total.astype(out.dtype)

        @pl.when(table[FACTS, CORE] != plain)
        def _():
            label = own[:1, :]
            theirs = arrival[length : length + LABEL, :].astype(jnp.float32)[:1, :]
            behind = next_orbs[0:1, 1:2].astype(jnp.float32)
            kept[...] = value + jnp.where(theirs == label, extra, 0.0)
            out[:length, :] = (
                jnp.where(label == behind, value, 0.0) + jnp.where(theirs == behind, extra, 0.0)
            ).astype(out.dtype)

    return pl.pallas_call(
        body,
        out_shape=[
            jax.ShapeDtypeStruct((length, LANES), jnp.float32),
            jax.ShapeDtypeStruct(arrival.shape, arrival.dtype),
        ],
        in_specs=[SMEM, VMEM, VMEM, VMEM],
        out_specs=[VMEM, VMEM],
        compiler_params=params(16),
        name="step",
    )(in_smem(table), next_orbs, mine, arrival)


def last_step(mine, arrival):
    length = mine.shape[0]

    def body(mine, arrival, out):
        out[...] = (mine[...] + arrival[:length, :].astype(jnp.float32)).astype(out.dtype)

    return pl.pallas_call(
        body,
        out_shape=jax.ShapeDtypeStruct(mine.shape, arrival.dtype),
        in_specs=[VMEM, VMEM],
        out_specs=VMEM,
        compiler_params=params(16),
        name="last_step",
    )(mine, arrival)


def ladder_build(table, held, factor):
    empty, tile = held.shape[0] - 1, held.shape[1]
    width = factor.shape[0]
    tiles = width // tile
    pairs = -(-tiles // 2)

    def body(table, held, source, left, factor, wide, state, sems):
        def load(c):
            here = block(c, tile)
            return pltpu.make_async_copy(source.at[:, here], factor.at[:, here], sems.at[c])

        def start(c):
            @pl.when(state[c] == 0)
            def _():
                load(c).start()
                state[c] = 1

        def wait(c):
            @pl.when(state[c] == 1)
            def _():
                load(c).wait()
                state[c] = 2

        for c in range(tiles):
            state[c] = 0
        used = table[FACTS, USED]
        kept = table[BEGIN, used]

        def start_slot(k, carry):
            start(table[COLUMN, table[SORTED, k]])
            return carry

        def start_rest(c, carry):
            start(c)
            return carry

        lax.fori_loop(0, kept, start_slot, 0)
        lax.fori_loop(0, tiles, start_rest, 0)

        def two_tiles(m, carry):
            first, second, end = [table[BEGIN, 2 * m + k] for k in range(3)]
            here = block(m, 2 * tile)

            def wait_slot(k, carry):
                wait(table[COLUMN, table[SORTED, k]])
                return carry

            lax.fori_loop(first, end, wait_slot, 0)

            def product(at, count):
                columns, weights = [], []
                for k in range(count):
                    there = at + k < end
                    s = table[SORTED, jnp.where(there, at + k, first)]
                    columns.append(factor[:, block(table[COLUMN, s], tile)])
                    value, none = held[jnp.where(there, s, empty)], jnp.zeros((tile, tile), held.dtype)
                    early = at + k < second
                    weights.append(
                        jnp.concatenate([jnp.where(early, value, none), jnp.where(early, none, value)], axis=1)
                    )
                return jnp.dot(
                    jnp.concatenate(columns, axis=1), jnp.concatenate(weights, axis=0),
                    preferred_element_type=jnp.float32,
                )

            rounds = (end - first + 1) // 2
            for n in range(1, 4):

                @pl.when(rounds == n)
                def _():
                    left[:, here] = product(first, 2 * n).astype(left.dtype)

            @pl.when(rounds > 3)
            def _():
                wide[...] = product(first, 2)

                def add(t, carry):
                    wide[...] += product(first + 2 * t, 2)
                    return carry

                lax.fori_loop(1, rounds, add, 0)
                left[:, here] = wide[...].astype(left.dtype)

            return carry

        lax.fori_loop(0, (used + 1) // 2, two_tiles, 0)

        def wait_rest(c, carry):
            wait(c)
            return carry

        lax.fori_loop(0, tiles, wait_rest, 0)

    return pl.pallas_call(
        body,
        out_shape=[
            jax.ShapeDtypeStruct((width, 2 * pairs * tile), jnp.bfloat16),
            jax.ShapeDtypeStruct(factor.shape, factor.dtype),
        ],
        in_specs=[SMEM, VMEM, HBM],
        out_specs=[VMEM, VMEM],
        scratch_shapes=[
            pltpu.VMEM((width, 2 * tile), jnp.float32),
            pltpu.SMEM((tiles,), jnp.int32),
            pltpu.SemaphoreType.DMA((tiles,)),
        ],
        compiler_params=params(32),
        cost_estimate=pl.CostEstimate(flops=10**10, bytes_accessed=1, transcendentals=0),
        name="ladder_build",
    )(in_smem(table), held, in_hbm(factor))


def ladder_multiply(table, left, factor, tile, *, far, flops):
    half = left.shape[0] // 2

    def body(table, left, factor, out):
        core = table[FACTS, CORE]
        rows = block(1 - core if far else core, half)
        steps = (table[FACTS, USED] + 1) // 2
        for n in range(factor.shape[0] // tile // 2 + 1):

            @pl.when(steps == n)
            def _():
                def unit(k, carry):
                    if n == 0:
                        out[k] = jnp.zeros((half, half), out.dtype)
                        return carry
                    here = block(k, half)
                    right = jnp.concatenate(
                        [factor[here, block(table[NAME, w], tile)] for w in range(2 * n)], axis=1
                    )
                    out[k] = lax.dot_general(
                        left[rows, : 2 * n * tile], right, LAST_LAST, preferred_element_type=jnp.float32
                    ).astype(out.dtype)
                    return carry

                lax.fori_loop(0, 2, unit, 0)

    return ladder_call(body, (2, half, half), [], in_smem(table), left, factor, flops=flops)


def ladder_call(body, shape, scratch, *operands, flops):
    return pl.pallas_call(
        body,
        out_shape=jax.ShapeDtypeStruct(shape, jnp.bfloat16),
        in_specs=[SMEM] + [VMEM] * (len(operands) - 1),
        out_specs=VMEM,
        scratch_shapes=scratch,
        compiler_params=params(32),
        cost_estimate=pl.CostEstimate(flops=flops, bytes_accessed=1, transcendentals=0),
        name="ladder",
    )(*operands)


def finish(table, sums, near, arrived, cycle_rows, whole, *, pieces):
    half = arrived.shape[1]
    aux = cycle_rows.shape[1]
    rows = half // pieces
    first = whole is None

    def body(table, sums, near, arrived, factor, *refs):
        out, low, done, sems = refs[-4:]
        core = table[FACTS, CORE]
        side = core if first else 1 - core
        for n in range(half // LANES):
            low[:, n * LANES : (n + 1) * LANES] = sums[n * aux : (n + 1) * aux, :]
        stores = []
        for n in range(pieces):
            here = slice(n * rows, (n + 1) * rows)
            term = jnp.dot(
                factor[pl.ds(pl.multiple_of(core * half + n * rows, rows), rows), :], low[...],
                preferred_element_type=jnp.float32,
            )
            ladder = near[side, here, :].astype(jnp.float32) + arrived[side, here, :].astype(jnp.float32)
            total = ladder + term
            done[here, :] = total.astype(done.dtype)
            store = pltpu.make_async_copy(
                done.at[here, :], out.at[here, block(side, half)], sems.at[n]
            )
            store.start()
            stores.append(store)
        for store in stores:
            store.wait()

    operands = [in_smem(table), sums, near, arrived, cycle_rows]
    return pl.pallas_call(
        body,
        out_shape=jax.ShapeDtypeStruct((half, 2 * half), jnp.bfloat16),
        in_specs=[SMEM] + [VMEM] * 4 + [HBM] * (not first),
        out_specs=HBM,
        scratch_shapes=[
            pltpu.VMEM((aux, half), jnp.bfloat16),
            pltpu.VMEM((half, half), jnp.bfloat16),
            pltpu.SemaphoreType.DMA((pieces,)),
        ],
        input_output_aliases={} if first else {len(operands): 0},
        compiler_params=params(16),
        cost_estimate=pl.CostEstimate(flops=10**9, bytes_accessed=1, transcendentals=0),
        name="finish_own" if first else "finish_other",
    )(*operands, *([] if first else [whole]))


def shards(amp_tiles, tile_coords, tile_mask, pair_orbs, ladder_factor, cycle_factor):
    cores, pairs = lax.axis_size("virt"), lax.axis_size("pair")
    assert cores == 2 and pairs % 2 == 0
    own = amp_tiles[0]
    place = lax.axis_index("virt").astype(jnp.int32).reshape(1)
    swap = [(0, 1), (1, 0)]
    other = lax.ppermute(own, "virt", swap)
    square = pairs == 8
    table, own, cycle_rows, start = prepare(tile_coords[0].T, tile_mask, pair_orbs, place, own, cycle_factor, cores=cores)
    message, held = intermediate(table, own, other, cycle_rows, start)
    factor = ladder_factor[0]
    tile = held.shape[1]

    def exchange(value, *partners):
        routes = [(p * 2 + c, (p ^ partners[c]) * 2 + c) for p in range(pairs) for c in range(2)]
        return lax.ppermute(value, ("pair", "virt"), routes)

    if square:
        arrival = exchange(message, ORDERS[0][0], ORDERS[1][0])
        message, pair_orbs, held, factor = lax.optimization_barrier((message, pair_orbs, held, factor))
        next_orbs = exchange(pair_orbs, ORDERS[0][2], ORDERS[1][1])
        left, factor = ladder_build(table, held, factor)
        arrival, left = lax.optimization_barrier((arrival, left))
        kept, message = step(table, next_orbs, message, arrival, plain=0)
        message, left = lax.optimization_barrier((message, left))
        arrival = exchange(message, ORDERS[0][1], ORDERS[1][1])
        far = ladder_multiply(table, left, factor, tile, far=True, flops=10**10)
        arrival, far = lax.optimization_barrier((arrival, far))
        kept, message = step(table, next_orbs, kept, arrival, plain=1)
        message, left, far = lax.optimization_barrier((message, left, far))
        arrival = exchange(message, ORDERS[0][2], ORDERS[1][2])
        arrived = lax.ppermute(far, "virt", swap)
        near = ladder_multiply(table, left, factor, tile, far=False, flops=4 * 10**10)
        arrival, near = lax.optimization_barrier((arrival, near))
        sums = last_step(kept, arrival)
    else:
        left, factor = ladder_build(table, held, factor)
        far = ladder_multiply(table, left, factor, tile, far=True, flops=10**10)
        near = ladder_multiply(table, left, factor, tile, far=False, flops=10**10)
        arrived = lax.ppermute(far, "virt", swap)
        right = pair_orbs[0, 1]
        occupied = jnp.arange(cycle_factor.shape[0], dtype=jnp.int32) == right
        mine = message[:-LABEL].astype(jnp.float32)
        total = lax.psum(jnp.where(occupied[:, None, None], mine[None], 0.0), "pair")
        sums = lax.dynamic_index_in_dim(total, right, 0, keepdims=False).astype(jnp.bfloat16)

    other_sums = lax.ppermute(sums, "virt", swap)
    own_side = finish(table, sums, near, arrived, cycle_rows, None, pieces=4)
    return finish(table, other_sums, near, arrived, cycle_rows, own_side, pieces=4)[None]


def solution(mesh):
    in_specs = (
        P(("groups", "pair"), "virt", None, None),
        P(("groups", "pair"), None, None),
        P(("groups", "pair"), None),
        P(("groups", "pair"), None),
        P(("groups", "virt"), None, None),
        P("groups", None, None),
    )
    out_specs = P(("groups", "pair"), "virt", None)
    return jax.shard_map(shards, mesh=mesh, in_specs=in_specs, out_specs=out_specs, check_vma=False)
```

```python
import functools

import jax
import jax.numpy as jnp
from jax import lax
from jax.experimental import pallas as pl
from jax.experimental.pallas import tpu as pltpu
from jax.sharding import PartitionSpec as P

LANES, LABEL = 128, 16
ORDERS = (4, 2, 1), (2, 1, 4)
SMEM = pl.BlockSpec(memory_space=pltpu.SMEM)
VMEM = pl.BlockSpec(memory_space=pltpu.VMEM)
HBM = pl.BlockSpec(memory_space=pltpu.HBM)
FIRST_FIRST = (((0,), (0,)), ((), ()))
LAST_LAST = (((1,), (1,)), ((), ()))
COLUMN, ROW, KEPT, SORTED, NAME, BEGIN, FACTS = range(7)
USED, CORE, ORBITAL = range(3)


def params(mib):
    return pltpu.CompilerParams(vmem_limit_bytes=mib * 2**20)


def block(index, size):
    return pl.ds(pl.multiple_of(index * size, size), size)


def in_hbm(array):
    return pltpu.with_memory_space_constraint(array, pltpu.HBM)


def in_smem(array):
    return pltpu.with_memory_space_constraint(array, pltpu.SMEM)


def add_terms(total, table, rows, tiles, slots):
    size = tiles.shape[1]
    terms = [
        lax.dot_general(
            rows[block(table[COLUMN, s], size), :], tiles[k], FIRST_FIRST, preferred_element_type=jnp.float32
        )
        for k, s in enumerate(slots)
    ]
    for s, term in zip(slots, terms):
        total[:, block(table[ROW, s], size)] += term * table[KEPT, s].astype(jnp.float32)


def prepare(coords, mask, orbs, place, own, cycle_factor, *, cores):
    slots = coords.shape[1]
    local, tile = own.shape[0], own.shape[1]
    width, aux = cycle_factor.shape[1:]
    tiles, tiles_here = width // tile, width // tile // cores
    places = max(slots + 1, tiles + 3)

    def body(coords, mask, orbs, place, own, factor, table, held, rows, total, s_coords, s_mask, count, sems):
        loads = [
            pltpu.make_async_copy(source, target, sems.at[n])
            for n, (source, target) in enumerate([(coords, s_coords), (mask, s_mask), (own, held)])
        ]
        for load in loads:
            load.start()
        core = place[0]
        total[...] = jnp.zeros_like(total)
        load_rows = pltpu.make_async_copy(factor.at[orbs[0, 0]], rows, sems.at[4])
        load_rows.start()
        table[FACTS, CORE] = core
        table[FACTS, ORBITAL] = orbs[0, 1]

        for n in range(tiles):
            count[n] = 0
        loads[0].wait()
        loads[1].wait()
        for s in range(slots):
            g = lax.rem(s + core * local, slots)
            d, kept = s_coords[1, g], s_mask[0, g]
            table[COLUMN, s] = s_coords[0, g]
            inside = d // tiles_here == core
            table[ROW, s] = jnp.where(inside, d - core * tiles_here, 0)
            table[KEPT, s] = jnp.where(inside, kept, 0)
            table[SORTED, s] = slots
            count[d] += (kept != 0).astype(jnp.int32)
        table[COLUMN, slots] = 0
        begin, used = jnp.int32(0), jnp.int32(0)
        for n in range(tiles):
            here = count[n]
            table[NAME, used] = n
            table[BEGIN, used] = begin
            count[n] = begin
            begin += here
            used += (here > 0).astype(jnp.int32)
        table[FACTS, USED] = used
        for n in range(3):
            table[NAME, used + n] = 0
            table[BEGIN, used + n] = begin
        for s in range(slots):
            g = lax.rem(s + core * local, slots)
            d, kept = s_coords[1, g], s_mask[0, g] != 0
            at = count[d]
            table[SORTED, jnp.where(kept, at, slots)] = s
            count[d] = at + kept.astype(jnp.int32)
        loads[2].wait()
        load_rows.wait()
        add_terms(total, table, rows, held, range(local))

    return pl.pallas_call(
        body,
        out_shape=[
            pltpu.SMEM((7, places), jnp.int32),
            jax.ShapeDtypeStruct(own.shape, own.dtype),
            jax.ShapeDtypeStruct((width, aux), jnp.bfloat16),
            jax.ShapeDtypeStruct((aux, width // cores), jnp.float32),
        ],
        in_specs=[HBM, HBM, SMEM, SMEM, HBM, HBM],
        out_specs=[SMEM, VMEM, VMEM, VMEM],
        scratch_shapes=[
            pltpu.SMEM(coords.shape, jnp.int32),
            pltpu.SMEM(mask.shape, jnp.int32),
            pltpu.SMEM((tiles,), jnp.int32),
            pltpu.SemaphoreType.DMA((5,)),
        ],
        compiler_params=params(16),
        name="prepare",
    )(in_hbm(coords), in_hbm(mask), in_smem(orbs), place, in_hbm(own), in_hbm(cycle_factor))


def intermediate(table, own, other, rows, start):
    local, tile = own.shape[0], own.shape[1]
    aux, width = start.shape
    blocks = width // LANES

    def body(table, own, other, rows, start, out, held, total):
        total[...] = start[...]
        add_terms(total, table, rows, other, range(local, 2 * local))
        for n in range(blocks):
            out[n * aux : (n + 1) * aux, :] = total[:, n * LANES : (n + 1) * LANES].astype(out.dtype)
        label = jnp.zeros((LABEL, LANES), jnp.float32) + table[FACTS, ORBITAL].astype(jnp.float32)
        out[blocks * aux :, :] = label.astype(out.dtype)
        held[:local] = own[...]
        held[local : 2 * local] = other[...]
        held[2 * local] = jnp.zeros((tile, tile), held.dtype)

    return pl.pallas_call(
        body,
        out_shape=[
            jax.ShapeDtypeStruct((blocks * aux + LABEL, LANES), jnp.bfloat16),
            jax.ShapeDtypeStruct((2 * local + 1, tile, tile), jnp.bfloat16),
        ],
        in_specs=[SMEM, VMEM, VMEM, VMEM, VMEM],
        out_specs=[VMEM, VMEM],
        scratch_shapes=[pltpu.VMEM((aux, width), jnp.float32)],
        compiler_params=params(16),
        name="intermediate",
    )(in_smem(table), own, other, rows, start)


def step(table, next_orbs, mine, arrival, *, plain):
    length = arrival.shape[0] - LABEL

    def body(table, next_orbs, mine, arrival, kept, out):
        value = mine[:length, :].astype(jnp.float32)
        extra = arrival[:length, :].astype(jnp.float32)
        own = jnp.zeros((LABEL, LANES), jnp.float32) + table[FACTS, ORBITAL].astype(jnp.float32)
        out[length:, :] = own.astype(out.dtype)

        @pl.when(table[FACTS, CORE] == plain)
        def _():
            total = value + extra
            kept[...] = total
            out[:length, :] = total.astype(out.dtype)

        @pl.when(table[FACTS, CORE] != plain)
        def _():
            label = own[:1, :]
            theirs = arrival[length : length + LABEL, :].astype(jnp.float32)[:1, :]
            behind = next_orbs[0:1, 1:2].astype(jnp.float32)
            kept[...] = value + jnp.where(theirs == label, extra, 0.0)
            out[:length, :] = (
                jnp.where(label == behind, value, 0.0) + jnp.where(theirs == behind, extra, 0.0)
            ).astype(out.dtype)

    return pl.pallas_call(
        body,
        out_shape=[
            jax.ShapeDtypeStruct((length, LANES), jnp.float32),
            jax.ShapeDtypeStruct(arrival.shape, arrival.dtype),
        ],
        in_specs=[SMEM, VMEM, VMEM, VMEM],
        out_specs=[VMEM, VMEM],
        compiler_params=params(16),
        name="step",
    )(in_smem(table), next_orbs, mine, arrival)


def last_step(mine, arrival):
    length = mine.shape[0]

    def body(mine, arrival, out):
        out[...] = (mine[...] + arrival[:length, :].astype(jnp.float32)).astype(out.dtype)

    return pl.pallas_call(
        body,
        out_shape=jax.ShapeDtypeStruct(mine.shape, arrival.dtype),
        in_specs=[VMEM, VMEM],
        out_specs=VMEM,
        compiler_params=params(16),
        name="last_step",
    )(mine, arrival)


def ladder_build(table, held, factor):
    empty, tile = held.shape[0] - 1, held.shape[1]
    width = factor.shape[0]
    tiles = width // tile
    pairs = -(-tiles // 2)

    def body(table, held, source, left, factor, wide, state, sems):
        def load(c):
            here = block(c, tile)
            return pltpu.make_async_copy(source.at[:, here], factor.at[:, here], sems.at[c])

        def start(c):
            @pl.when(state[c] == 0)
            def _():
                load(c).start()
                state[c] = 1

        def wait(c):
            @pl.when(state[c] == 1)
            def _():
                load(c).wait()
                state[c] = 2

        for c in range(tiles):
            state[c] = 0
        used = table[FACTS, USED]
        kept = table[BEGIN, used]

        def start_slot(k, carry):
            start(table[COLUMN, table[SORTED, k]])
            return carry

        def start_rest(c, carry):
            start(c)
            return carry

        lax.fori_loop(0, kept, start_slot, 0)
        lax.fori_loop(0, tiles, start_rest, 0)

        def two_tiles(m, carry):
            first, second, end = [table[BEGIN, 2 * m + k] for k in range(3)]
            here = block(m, 2 * tile)

            def wait_slot(k, carry):
                wait(table[COLUMN, table[SORTED, k]])
                return carry

            lax.fori_loop(first, end, wait_slot, 0)

            def product(at, count):
                columns, weights = [], []
                for k in range(count):
                    there = at + k < end
                    s = table[SORTED, jnp.where(there, at + k, first)]
                    columns.append(factor[:, block(table[COLUMN, s], tile)])
                    value, none = held[jnp.where(there, s, empty)], jnp.zeros((tile, tile), held.dtype)
                    early = at + k < second
                    weights.append(
                        jnp.concatenate([jnp.where(early, value, none), jnp.where(early, none, value)], axis=1)
                    )
                return jnp.dot(
                    jnp.concatenate(columns, axis=1), jnp.concatenate(weights, axis=0),
                    preferred_element_type=jnp.float32,
                )

            rounds = (end - first + 1) // 2
            for n in range(1, 4):

                @pl.when(rounds == n)
                def _():
                    left[:, here] = product(first, 2 * n).astype(left.dtype)

            @pl.when(rounds > 3)
            def _():
                wide[...] = product(first, 2)

                def add(t, carry):
                    wide[...] += product(first + 2 * t, 2)
                    return carry

                lax.fori_loop(1, rounds, add, 0)
                left[:, here] = wide[...].astype(left.dtype)

            return carry

        lax.fori_loop(0, (used + 1) // 2, two_tiles, 0)

        def wait_rest(c, carry):
            wait(c)
            return carry

        lax.fori_loop(0, tiles, wait_rest, 0)

    return pl.pallas_call(
        body,
        out_shape=[
            jax.ShapeDtypeStruct((width, 2 * pairs * tile), jnp.bfloat16),
            jax.ShapeDtypeStruct(factor.shape, factor.dtype),
        ],
        in_specs=[SMEM, VMEM, HBM],
        out_specs=[VMEM, VMEM],
        scratch_shapes=[
            pltpu.VMEM((width, 2 * tile), jnp.float32),
            pltpu.SMEM((tiles,), jnp.int32),
            pltpu.SemaphoreType.DMA((tiles,)),
        ],
        compiler_params=params(32),
        cost_estimate=pl.CostEstimate(flops=10**10, bytes_accessed=1, transcendentals=0),
        name="ladder_build",
    )(in_smem(table), held, in_hbm(factor))


def ladder_multiply(table, left, factor, tile, *, far, flops):
    half = left.shape[0] // 2

    def body(table, left, factor, out):
        core = table[FACTS, CORE]
        rows = block(1 - core if far else core, half)
        steps = (table[FACTS, USED] + 1) // 2
        for n in range(factor.shape[0] // tile // 2 + 1):

            @pl.when(steps == n)
            def _():
                def unit(k, carry):
                    if n == 0:
                        out[k] = jnp.zeros((half, half), out.dtype)
                        return carry
                    here = block(k, half)
                    right = jnp.concatenate(
                        [factor[here, block(table[NAME, w], tile)] for w in range(2 * n)], axis=1
                    )
                    out[k] = lax.dot_general(
                        left[rows, : 2 * n * tile], right, LAST_LAST, preferred_element_type=jnp.float32
                    ).astype(out.dtype)
                    return carry

                lax.fori_loop(0, 2, unit, 0)

    return ladder_call(body, (2, half, half), [], in_smem(table), left, factor, flops=flops)


def ladder_call(body, shape, scratch, *operands, flops):
    return pl.pallas_call(
        body,
        out_shape=jax.ShapeDtypeStruct(shape, jnp.bfloat16),
        in_specs=[SMEM] + [VMEM] * (len(operands) - 1),
        out_specs=VMEM,
        scratch_shapes=scratch,
        compiler_params=params(32),
        cost_estimate=pl.CostEstimate(flops=flops, bytes_accessed=1, transcendentals=0),
        name="ladder",
    )(*operands)


def finish(table, sums, near, arrived, cycle_rows, whole, *, pieces):
    half = arrived.shape[1]
    aux = cycle_rows.shape[1]
    rows = half // pieces
    first = whole is None

    def body(table, sums, near, arrived, factor, *refs):
        out, low, done, sems = refs[-4:]
        core = table[FACTS, CORE]
        side = core if first else 1 - core
        for n in range(half // LANES):
            low[:, n * LANES : (n + 1) * LANES] = sums[n * aux : (n + 1) * aux, :]
        stores = []
        for n in range(pieces):
            here = slice(n * rows, (n + 1) * rows)
            term = jnp.dot(
                factor[pl.ds(pl.multiple_of(core * half + n * rows, rows), rows), :], low[...],
                preferred_element_type=jnp.float32,
            )
            ladder = near[side, here, :].astype(jnp.float32) + arrived[side, here, :].astype(jnp.float32)
            total = ladder + term
            done[here, :] = total.astype(done.dtype)
            store = pltpu.make_async_copy(
                done.at[here, :], out.at[here, block(side, half)], sems.at[n]
            )
            store.start()
            stores.append(store)
        for store in stores:
            store.wait()

    operands = [in_smem(table), sums, near, arrived, cycle_rows]
    return pl.pallas_call(
        body,
        out_shape=jax.ShapeDtypeStruct((half, 2 * half), jnp.bfloat16),
        in_specs=[SMEM] + [VMEM] * 4 + [HBM] * (not first),
        out_specs=HBM,
        scratch_shapes=[
            pltpu.VMEM((aux, half), jnp.bfloat16),
            pltpu.VMEM((half, half), jnp.bfloat16),
            pltpu.SemaphoreType.DMA((pieces,)),
        ],
        input_output_aliases={} if first else {len(operands): 0},
        compiler_params=params(16),
        cost_estimate=pl.CostEstimate(flops=10**9, bytes_accessed=1, transcendentals=0),
        name="finish_own" if first else "finish_other",
    )(*operands, *([] if first else [whole]))


def shards(amp_tiles, tile_coords, tile_mask, pair_orbs, ladder_factor, cycle_factor):
    cores, pairs = lax.axis_size("virt"), lax.axis_size("pair")
    assert cores == 2 and pairs % 2 == 0
    own = amp_tiles[0]
    place = lax.axis_index("virt").astype(jnp.int32).reshape(1)
    swap = [(0, 1), (1, 0)]
    other = lax.ppermute(own, "virt", swap)
    square = pairs == 8
    table, own, cycle_rows, start = prepare(tile_coords[0].T, tile_mask, pair_orbs, place, own, cycle_factor, cores=cores)
    message, held = intermediate(table, own, other, cycle_rows, start)
    factor = ladder_factor[0]
    tile = held.shape[1]

    def exchange(value, *partners):
        routes = [(p * 2 + c, (p ^ partners[c]) * 2 + c) for p in range(pairs) for c in range(2)]
        return lax.ppermute(value, ("pair", "virt"), routes)

    if square:
        arrival = exchange(message, ORDERS[0][0], ORDERS[1][0])
        message, pair_orbs, held, factor = lax.optimization_barrier((message, pair_orbs, held, factor))
        next_orbs = exchange(pair_orbs, ORDERS[0][2], ORDERS[1][1])
        left, factor = ladder_build(table, held, factor)
        arrival, left = lax.optimization_barrier((arrival, left))
        kept, message = step(table, next_orbs, message, arrival, plain=0)
        message, left = lax.optimization_barrier((message, left))
        arrival = exchange(message, ORDERS[0][1], ORDERS[1][1])
        far = ladder_multiply(table, left, factor, tile, far=True, flops=10**10)
        arrival, far = lax.optimization_barrier((arrival, far))
        kept, message = step(table, next_orbs, kept, arrival, plain=1)
        message, left, far = lax.optimization_barrier((message, left, far))
        arrival = exchange(message, ORDERS[0][2], ORDERS[1][2])
        arrived = lax.ppermute(far, "virt", swap)
        near = ladder_multiply(table, left, factor, tile, far=False, flops=4 * 10**10)
        arrival, near = lax.optimization_barrier((arrival, near))
        sums = last_step(kept, arrival)
    else:
        left, factor = ladder_build(table, held, factor)
        far = ladder_multiply(table, left, factor, tile, far=True, flops=10**10)
        near = ladder_multiply(table, left, factor, tile, far=False, flops=10**10)
        arrived = lax.ppermute(far, "virt", swap)
        right = pair_orbs[0, 1]
        occupied = jnp.arange(cycle_factor.shape[0], dtype=jnp.int32) == right
        mine = message[:-LABEL].astype(jnp.float32)
        total = lax.psum(jnp.where(occupied[:, None, None], mine[None], 0.0), "pair")
        sums = lax.dynamic_index_in_dim(total, right, 0, keepdims=False).astype(jnp.bfloat16)

    other_sums = lax.ppermute(sums, "virt", swap)
    own_side = finish(table, sums, near, arrived, cycle_rows, None, pieces=4)
    return finish(table, other_sums, near, arrived, cycle_rows, own_side, pieces=4)[None]


def solution(mesh):
    in_specs = (
        P(("groups", "pair"), "virt", None, None),
        P(("groups", "pair"), None, None),
        P(("groups", "pair"), None),
        P(("groups", "pair"), None),
        P(("groups", "virt"), None, None),
        P("groups", None, None),
    )
    out_specs = P(("groups", "pair"), "virt", None)
    return jax.shard_map(shards, mesh=mesh, in_specs=in_specs, out_specs=out_specs, check_vma=False)
```

```python
import functools

import jax
import jax.numpy as jnp
from jax import lax
from jax.experimental import pallas as pl
from jax.experimental.pallas import tpu as pltpu
from jax.sharding import PartitionSpec as P

LANES, LABEL = 128, 16
ORDERS = (4, 2, 1), (2, 1, 4)
SMEM = pl.BlockSpec(memory_space=pltpu.SMEM)
VMEM = pl.BlockSpec(memory_space=pltpu.VMEM)
HBM = pl.BlockSpec(memory_space=pltpu.HBM)
FIRST_FIRST = (((0,), (0,)), ((), ()))
LAST_LAST = (((1,), (1,)), ((), ()))
COLUMN, ROW, KEPT, SORTED, NAME, BEGIN, FACTS = range(7)
USED, CORE, ORBITAL = range(3)


def params(mib):
    return pltpu.CompilerParams(vmem_limit_bytes=mib * 2**20)


def block(index, size):
    return pl.ds(pl.multiple_of(index * size, size), size)


def in_hbm(array):
    return pltpu.with_memory_space_constraint(array, pltpu.HBM)


def in_smem(array):
    return pltpu.with_memory_space_constraint(array, pltpu.SMEM)


def add_terms(total, table, rows, tiles, slots):
    size = tiles.shape[1]
    terms = [
        lax.dot_general(
            rows[block(table[COLUMN, s], size), :], tiles[k], FIRST_FIRST, preferred_element_type=jnp.float32
        )
        for k, s in enumerate(slots)
    ]
    for s, term in zip(slots, terms):
        total[:, block(table[ROW, s], size)] += term * table[KEPT, s].astype(jnp.float32)


def prepare(coords, mask, orbs, place, own, cycle_factor, *, cores):
    slots = coords.shape[1]
    local, tile = own.shape[0], own.shape[1]
    width, aux = cycle_factor.shape[1:]
    tiles, tiles_here = width // tile, width // tile // cores
    places = max(slots + 1, tiles + 3)

    def body(coords, mask, orbs, place, own, factor, table, held, rows, total, s_coords, s_mask, s_orbs, count, sems):
        loads = [
            pltpu.make_async_copy(source, target, sems.at[n])
            for n, (source, target) in enumerate([(orbs, s_orbs), (coords, s_coords), (mask, s_mask), (own, held)])
        ]
        for load in loads:
            load.start()
        core = place[0]
        total[...] = jnp.zeros_like(total)
        loads[0].wait()
        load_rows = pltpu.make_async_copy(factor.at[s_orbs[0, 0]], rows, sems.at[4])
        load_rows.start()
        table[FACTS, CORE] = core
        table[FACTS, ORBITAL] = s_orbs[0, 1]

        for n in range(tiles):
            count[n] = 0
        loads[1].wait()
        loads[2].wait()
        for s in range(slots):
            g = lax.rem(s + core * local, slots)
            d, kept = s_coords[1, g], s_mask[0, g]
            table[COLUMN, s] = s_coords[0, g]
            inside = d // tiles_here == core
            table[ROW, s] = jnp.where(inside, d - core * tiles_here, 0)
            table[KEPT, s] = jnp.where(inside, kept, 0)
            table[SORTED, s] = slots
            count[d] += (kept != 0).astype(jnp.int32)
        table[COLUMN, slots] = 0
        begin, used = jnp.int32(0), jnp.int32(0)
        for n in range(tiles):
            here = count[n]
            table[NAME, used] = n
            table[BEGIN, used] = begin
            count[n] = begin
            begin += here
            used += (here > 0).astype(jnp.int32)
        table[FACTS, USED] = used
        for n in range(3):
            table[NAME, used + n] = 0
            table[BEGIN, used + n] = begin
        for s in range(slots):
            g = lax.rem(s + core * local, slots)
            d, kept = s_coords[1, g], s_mask[0, g] != 0
            at = count[d]
            table[SORTED, jnp.where(kept, at, slots)] = s
            count[d] = at + kept.astype(jnp.int32)
        loads[3].wait()
        load_rows.wait()
        add_terms(total, table, rows, held, range(local))

    return pl.pallas_call(
        body,
        out_shape=[
            pltpu.SMEM((7, places), jnp.int32),
            jax.ShapeDtypeStruct(own.shape, own.dtype),
            jax.ShapeDtypeStruct((width, aux), jnp.bfloat16),
            jax.ShapeDtypeStruct((aux, width // cores), jnp.float32),
        ],
        in_specs=[HBM, HBM, HBM, SMEM, HBM, HBM],
        out_specs=[SMEM, VMEM, VMEM, VMEM],
        scratch_shapes=[
            pltpu.SMEM(coords.shape, jnp.int32),
            pltpu.SMEM(mask.shape, jnp.int32),
            pltpu.SMEM(orbs.shape, jnp.int32),
            pltpu.SMEM((tiles,), jnp.int32),
            pltpu.SemaphoreType.DMA((5,)),
        ],
        compiler_params=params(16),
        name="prepare",
    )(in_hbm(coords), in_hbm(mask), in_hbm(orbs), place, in_hbm(own), in_hbm(cycle_factor))


def intermediate(table, own, other, rows, start):
    local = own.shape[0]
    aux, width = start.shape
    blocks = width // LANES

    def body(table, own, other, rows, start, out, total):
        total[...] = start[...]
        add_terms(total, table, rows, other, range(local, 2 * local))
        for n in range(blocks):
            out[n * aux : (n + 1) * aux, :] = total[:, n * LANES : (n + 1) * LANES].astype(out.dtype)
        label = jnp.zeros((LABEL, LANES), jnp.float32) + table[FACTS, ORBITAL].astype(jnp.float32)
        out[blocks * aux :, :] = label.astype(out.dtype)

    return pl.pallas_call(
        body,
        out_shape=jax.ShapeDtypeStruct((blocks * aux + LABEL, LANES), jnp.bfloat16),
        in_specs=[SMEM, VMEM, VMEM, VMEM, VMEM],
        out_specs=VMEM,
        scratch_shapes=[pltpu.VMEM((aux, width), jnp.float32)],
        compiler_params=params(16),
        name="intermediate",
    )(in_smem(table), own, other, rows, start)


def step(table, next_orbs, mine, arrival, *, plain):
    length = arrival.shape[0] - LABEL

    def body(table, next_orbs, mine, arrival, kept, out):
        value = mine[:length, :].astype(jnp.float32)
        extra = arrival[:length, :].astype(jnp.float32)
        own = jnp.zeros((LABEL, LANES), jnp.float32) + table[FACTS, ORBITAL].astype(jnp.float32)
        out[length:, :] = own.astype(out.dtype)

        @pl.when(table[FACTS, CORE] == plain)
        def _():
            total = value + extra
            kept[...] = total
            out[:length, :] = total.astype(out.dtype)

        @pl.when(table[FACTS, CORE] != plain)
        def _():
            label = own[:1, :]
            theirs = arrival[length : length + LABEL, :].astype(jnp.float32)[:1, :]
            behind = next_orbs[0:1, 1:2].astype(jnp.float32)
            kept[...] = value + jnp.where(theirs == label, extra, 0.0)
            out[:length, :] = (
                jnp.where(label == behind, value, 0.0) + jnp.where(theirs == behind, extra, 0.0)
            ).astype(out.dtype)

    return pl.pallas_call(
        body,
        out_shape=[
            jax.ShapeDtypeStruct((length, LANES), jnp.float32),
            jax.ShapeDtypeStruct(arrival.shape, arrival.dtype),
        ],
        in_specs=[SMEM, VMEM, VMEM, VMEM],
        out_specs=[VMEM, VMEM],
        compiler_params=params(16),
        name="step",
    )(in_smem(table), next_orbs, mine, arrival)


def last_step(mine, arrival):
    length = mine.shape[0]

    def body(mine, arrival, out):
        out[...] = (mine[...] + arrival[:length, :].astype(jnp.float32)).astype(out.dtype)

    return pl.pallas_call(
        body,
        out_shape=jax.ShapeDtypeStruct(mine.shape, arrival.dtype),
        in_specs=[VMEM, VMEM],
        out_specs=VMEM,
        compiler_params=params(16),
        name="last_step",
    )(mine, arrival)


def ladder_build(table, own, other, factor):
    local, tile = own.shape[0], own.shape[1]
    empty = 2 * local
    width = factor.shape[0]
    tiles = width // tile
    pairs = -(-tiles // 2)

    def body(table, own, other, source, left, factor, held, wide, state, sems):
        def load(c):
            here = block(c, tile)
            return pltpu.make_async_copy(source.at[:, here], factor.at[:, here], sems.at[c])

        def start(c):
            @pl.when(state[c] == 0)
            def _():
                load(c).start()
                state[c] = 1

        def wait(c):
            @pl.when(state[c] == 1)
            def _():
                load(c).wait()
                state[c] = 2

        for c in range(tiles):
            state[c] = 0
        used = table[FACTS, USED]
        kept = table[BEGIN, used]

        def start_slot(k, carry):
            start(table[COLUMN, table[SORTED, k]])
            return carry

        def start_rest(c, carry):
            start(c)
            return carry

        lax.fori_loop(0, kept, start_slot, 0)
        lax.fori_loop(0, tiles, start_rest, 0)
        held[:local] = own[...]
        held[local:empty] = other[...]
        held[empty] = jnp.zeros((tile, tile), held.dtype)

        def two_tiles(m, carry):
            first, second, end = [table[BEGIN, 2 * m + k] for k in range(3)]
            here = block(m, 2 * tile)

            def wait_slot(k, carry):
                wait(table[COLUMN, table[SORTED, k]])
                return carry

            lax.fori_loop(first, end, wait_slot, 0)

            def product(at, count):
                columns, weights = [], []
                for k in range(count):
                    there = at + k < end
                    s = table[SORTED, jnp.where(there, at + k, first)]
                    columns.append(factor[:, block(table[COLUMN, s], tile)])
                    value, none = held[jnp.where(there, s, empty)], jnp.zeros((tile, tile), held.dtype)
                    early = at + k < second
                    weights.append(
                        jnp.concatenate([jnp.where(early, value, none), jnp.where(early, none, value)], axis=1)
                    )
                return jnp.dot(
                    jnp.concatenate(columns, axis=1), jnp.concatenate(weights, axis=0),
                    preferred_element_type=jnp.float32,
                )

            rounds = (end - first + 1) // 2
            for n in range(1, 4):

                @pl.when(rounds == n)
                def _():
                    left[:, here] = product(first, 2 * n).astype(left.dtype)

            @pl.when(rounds > 3)
            def _():
                wide[...] = product(first, 2)

                def add(t, carry):
                    wide[...] += product(first + 2 * t, 2)
                    return carry

                lax.fori_loop(1, rounds, add, 0)
                left[:, here] = wide[...].astype(left.dtype)

            return carry

        lax.fori_loop(0, (used + 1) // 2, two_tiles, 0)

        def wait_rest(c, carry):
            wait(c)
            return carry

        lax.fori_loop(0, tiles, wait_rest, 0)

    return pl.pallas_call(
        body,
        out_shape=[
            jax.ShapeDtypeStruct((width, 2 * pairs * tile), jnp.bfloat16),
            jax.ShapeDtypeStruct(factor.shape, factor.dtype),
        ],
        in_specs=[SMEM, VMEM, VMEM, HBM],
        out_specs=[VMEM, VMEM],
        scratch_shapes=[
            pltpu.VMEM((empty + 1, tile, tile), own.dtype),
            pltpu.VMEM((width, 2 * tile), jnp.float32),
            pltpu.SMEM((tiles,), jnp.int32),
            pltpu.SemaphoreType.DMA((tiles,)),
        ],
        compiler_params=params(32),
        cost_estimate=pl.CostEstimate(flops=10**10, bytes_accessed=1, transcendentals=0),
        name="ladder_build",
    )(in_smem(table), own, other, in_hbm(factor))


def ladder_multiply(table, left, factor, tile, *, far, flops):
    half = left.shape[0] // 2

    def body(table, left, factor, out):
        core = table[FACTS, CORE]
        rows = block(1 - core if far else core, half)
        steps = (table[FACTS, USED] + 1) // 2
        for n in range(factor.shape[0] // tile // 2 + 1):

            @pl.when(steps == n)
            def _():
                def unit(k, carry):
                    if n == 0:
                        out[k] = jnp.zeros((half, half), out.dtype)
                        return carry
                    here = block(k, half)
                    right = jnp.concatenate(
                        [factor[here, block(table[NAME, w], tile)] for w in range(2 * n)], axis=1
                    )
                    out[k] = lax.dot_general(
                        left[rows, : 2 * n * tile], right, LAST_LAST, preferred_element_type=jnp.float32
                    ).astype(out.dtype)
                    return carry

                lax.fori_loop(0, 2, unit, 0)

    return ladder_call(body, (2, half, half), [], in_smem(table), left, factor, flops=flops)


def ladder_call(body, shape, scratch, *operands, flops):
    return pl.pallas_call(
        body,
        out_shape=jax.ShapeDtypeStruct(shape, jnp.bfloat16),
        in_specs=[SMEM] + [VMEM] * (len(operands) - 1),
        out_specs=VMEM,
        scratch_shapes=scratch,
        compiler_params=params(32),
        cost_estimate=pl.CostEstimate(flops=flops, bytes_accessed=1, transcendentals=0),
        name="ladder",
    )(*operands)


def finish(table, sums, near, arrived, cycle_rows, whole, *, pieces):
    half = arrived.shape[1]
    aux = cycle_rows.shape[1]
    rows = half // pieces
    first = whole is None

    def body(table, sums, near, arrived, factor, *refs):
        out, low, done, sems = refs[-4:]
        core = table[FACTS, CORE]
        side = core if first else 1 - core
        for n in range(half // LANES):
            low[:, n * LANES : (n + 1) * LANES] = sums[n * aux : (n + 1) * aux, :]
        stores = []
        for n in range(pieces):
            here = slice(n * rows, (n + 1) * rows)
            term = jnp.dot(
                factor[pl.ds(pl.multiple_of(core * half + n * rows, rows), rows), :], low[...],
                preferred_element_type=jnp.float32,
            )
            ladder = near[side, here, :].astype(jnp.float32) + arrived[side, here, :].astype(jnp.float32)
            total = ladder + term
            done[here, :] = total.astype(done.dtype)
            store = pltpu.make_async_copy(
                done.at[here, :], out.at[here, block(side, half)], sems.at[n]
            )
            store.start()
            stores.append(store)
        for store in stores:
            store.wait()

    operands = [in_smem(table), sums, near, arrived, cycle_rows]
    return pl.pallas_call(
        body,
        out_shape=jax.ShapeDtypeStruct((half, 2 * half), jnp.bfloat16),
        in_specs=[SMEM] + [VMEM] * 4 + [HBM] * (not first),
        out_specs=HBM,
        scratch_shapes=[
            pltpu.VMEM((aux, half), jnp.bfloat16),
            pltpu.VMEM((half, half), jnp.bfloat16),
            pltpu.SemaphoreType.DMA((pieces,)),
        ],
        input_output_aliases={} if first else {len(operands): 0},
        compiler_params=params(16),
        cost_estimate=pl.CostEstimate(flops=10**9, bytes_accessed=1, transcendentals=0),
        name="finish_own" if first else "finish_other",
    )(*operands, *([] if first else [whole]))


def shards(amp_tiles, tile_coords, tile_mask, pair_orbs, ladder_factor, cycle_factor):
    cores, pairs = lax.axis_size("virt"), lax.axis_size("pair")
    assert cores == 2 and pairs % 2 == 0
    own = amp_tiles[0]
    place = lax.axis_index("virt").astype(jnp.int32).reshape(1)
    swap = [(0, 1), (1, 0)]
    other = lax.ppermute(own, "virt", swap)
    square = pairs == 8
    table, own, cycle_rows, start = prepare(tile_coords[0].T, tile_mask, pair_orbs, place, own, cycle_factor, cores=cores)
    message = intermediate(table, own, other, cycle_rows, start)
    factor = ladder_factor[0]
    tile = own.shape[1]

    def exchange(value, *partners):
        routes = [(p * 2 + c, (p ^ partners[c]) * 2 + c) for p in range(pairs) for c in range(2)]
        return lax.ppermute(value, ("pair", "virt"), routes)

    if square:
        arrival = exchange(message, ORDERS[0][0], ORDERS[1][0])
        message, pair_orbs, own, other, factor = lax.optimization_barrier((message, pair_orbs, own, other, factor))
        next_orbs = exchange(pair_orbs, ORDERS[0][2], ORDERS[1][1])
        left, factor = ladder_build(table, own, other, factor)
        arrival, left = lax.optimization_barrier((arrival, left))
        kept, message = step(table, next_orbs, message, arrival, plain=0)
        message, left = lax.optimization_barrier((message, left))
        arrival = exchange(message, ORDERS[0][1], ORDERS[1][1])
        far = ladder_multiply(table, left, factor, tile, far=True, flops=10**10)
        arrival, far = lax.optimization_barrier((arrival, far))
        kept, message = step(table, next_orbs, kept, arrival, plain=1)
        message, left, far = lax.optimization_barrier((message, left, far))
        arrival = exchange(message, ORDERS[0][2], ORDERS[1][2])
        arrived = lax.ppermute(far, "virt", swap)
        near = ladder_multiply(table, left, factor, tile, far=False, flops=4 * 10**10)
        arrival, near = lax.optimization_barrier((arrival, near))
        sums = last_step(kept, arrival)
    else:
        left, factor = ladder_build(table, own, other, factor)
        far = ladder_multiply(table, left, factor, tile, far=True, flops=10**10)
        near = ladder_multiply(table, left, factor, tile, far=False, flops=10**10)
        arrived = lax.ppermute(far, "virt", swap)
        right = pair_orbs[0, 1]
        occupied = jnp.arange(cycle_factor.shape[0], dtype=jnp.int32) == right
        mine = message[:-LABEL].astype(jnp.float32)
        total = lax.psum(jnp.where(occupied[:, None, None], mine[None], 0.0), "pair")
        sums = lax.dynamic_index_in_dim(total, right, 0, keepdims=False).astype(jnp.bfloat16)

    other_sums = lax.ppermute(sums, "virt", swap)
    own_side = finish(table, sums, near, arrived, cycle_rows, None, pieces=4)
    return finish(table, other_sums, near, arrived, cycle_rows, own_side, pieces=4)[None]


def solution(mesh):
    in_specs = (
        P(("groups", "pair"), "virt", None, None),
        P(("groups", "pair"), None, None),
        P(("groups", "pair"), None),
        P(("groups", "pair"), None),
        P(("groups", "virt"), None, None),
        P("groups", None, None),
    )
    out_specs = P(("groups", "pair"), "virt", None)
    return jax.shard_map(shards, mesh=mesh, in_specs=in_specs, out_specs=out_specs, check_vma=False)
```

```python
import functools

import jax
import jax.numpy as jnp
from jax import lax
from jax.experimental import pallas as pl
from jax.experimental.pallas import tpu as pltpu
from jax.sharding import PartitionSpec as P

LANES, LABEL = 128, 16
ORDERS = (4, 2, 1), (2, 1, 4)
SMEM = pl.BlockSpec(memory_space=pltpu.SMEM)
VMEM = pl.BlockSpec(memory_space=pltpu.VMEM)
HBM = pl.BlockSpec(memory_space=pltpu.HBM)
FIRST_FIRST = (((0,), (0,)), ((), ()))
LAST_LAST = (((1,), (1,)), ((), ()))
COLUMN, ROW, KEPT, SORTED, NAME, BEGIN, FACTS = range(7)
USED, CORE, ORBITAL = range(3)


def params(mib):
    return pltpu.CompilerParams(vmem_limit_bytes=mib * 2**20)


def block(index, size):
    return pl.ds(pl.multiple_of(index * size, size), size)


def in_hbm(array):
    return pltpu.with_memory_space_constraint(array, pltpu.HBM)


def in_smem(array):
    return pltpu.with_memory_space_constraint(array, pltpu.SMEM)


def add_terms(total, table, rows, tiles, slots):
    size = tiles.shape[1]
    terms = [
        lax.dot_general(
            rows[block(table[COLUMN, s], size), :], tiles[k], FIRST_FIRST, preferred_element_type=jnp.float32
        )
        for k, s in enumerate(slots)
    ]
    for s, term in zip(slots, terms):
        total[:, block(table[ROW, s], size)] += term * table[KEPT, s].astype(jnp.float32)


def prepare(coords, mask, orbs, place, own, cycle_factor, *, cores):
    slots = coords.shape[1]
    local, tile = own.shape[0], own.shape[1]
    width, aux = cycle_factor.shape[1:]
    tiles, tiles_here = width // tile, width // tile // cores
    places = max(slots + 1, tiles + 3)

    def body(coords, mask, orbs, place, own, factor, table, held, rows, total, s_coords, s_mask, s_orbs, count, sems):
        loads = [
            pltpu.make_async_copy(source, target, sems.at[n])
            for n, (source, target) in enumerate([(orbs, s_orbs), (coords, s_coords), (mask, s_mask), (own, held)])
        ]
        for load in loads:
            load.start()
        core = place[0]
        total[...] = jnp.zeros_like(total)
        loads[0].wait()
        load_rows = pltpu.make_async_copy(factor.at[s_orbs[0, 0]], rows, sems.at[4])
        load_rows.start()
        table[FACTS, CORE] = core
        table[FACTS, ORBITAL] = s_orbs[0, 1]

        for n in range(tiles):
            count[n] = 0
        loads[1].wait()
        loads[2].wait()
        for s in range(slots):
            g = lax.rem(s + core * local, slots)
            d, kept = s_coords[1, g], s_mask[0, g]
            table[COLUMN, s] = s_coords[0, g]
            inside = d // tiles_here == core
            table[ROW, s] = jnp.where(inside, d - core * tiles_here, 0)
            table[KEPT, s] = jnp.where(inside, kept, 0)
            table[SORTED, s] = slots
            count[d] += (kept != 0).astype(jnp.int32)
        table[COLUMN, slots] = 0
        begin, used = jnp.int32(0), jnp.int32(0)
        for n in range(tiles):
            here = count[n]
            table[NAME, used] = n
            table[BEGIN, used] = begin
            count[n] = begin
            begin += here
            used += (here > 0).astype(jnp.int32)
        table[FACTS, USED] = used
        for n in range(3):
            table[NAME, used + n] = 0
            table[BEGIN, used + n] = begin
        for s in range(slots):
            g = lax.rem(s + core * local, slots)
            d, kept = s_coords[1, g], s_mask[0, g] != 0
            at = count[d]
            table[SORTED, jnp.where(kept, at, slots)] = s
            count[d] = at + kept.astype(jnp.int32)
        loads[3].wait()
        load_rows.wait()
        add_terms(total, table, rows, held, range(local))

    return pl.pallas_call(
        body,
        out_shape=[
            pltpu.SMEM((7, places), jnp.int32),
            jax.ShapeDtypeStruct(own.shape, own.dtype),
            jax.ShapeDtypeStruct((width, aux), jnp.bfloat16),
            jax.ShapeDtypeStruct((aux, width // cores), jnp.float32),
        ],
        in_specs=[HBM, HBM, HBM, SMEM, HBM, HBM],
        out_specs=[SMEM, VMEM, VMEM, VMEM],
        scratch_shapes=[
            pltpu.SMEM(coords.shape, jnp.int32),
            pltpu.SMEM(mask.shape, jnp.int32),
            pltpu.SMEM(orbs.shape, jnp.int32),
            pltpu.SMEM((tiles,), jnp.int32),
            pltpu.SemaphoreType.DMA((5,)),
        ],
        compiler_params=params(16),
        name="prepare",
    )(in_hbm(coords), in_hbm(mask), in_hbm(orbs), place, in_hbm(own), in_hbm(cycle_factor))


def intermediate(table, own, other, rows, start):
    local, tile = own.shape[0], own.shape[1]
    aux, width = start.shape
    blocks = width // LANES

    def body(table, own, other, rows, start, out, held, total):
        total[...] = start[...]
        add_terms(total, table, rows, other, range(local, 2 * local))
        for n in range(blocks):
            out[n * aux : (n + 1) * aux, :] = total[:, n * LANES : (n + 1) * LANES].astype(out.dtype)
        label = jnp.zeros((LABEL, LANES), jnp.float32) + table[FACTS, ORBITAL].astype(jnp.float32)
        out[blocks * aux :, :] = label.astype(out.dtype)
        held[:local] = own[...]
        held[local : 2 * local] = other[...]
        held[2 * local] = jnp.zeros((tile, tile), held.dtype)

    return pl.pallas_call(
        body,
        out_shape=[
            jax.ShapeDtypeStruct((blocks * aux + LABEL, LANES), jnp.bfloat16),
            jax.ShapeDtypeStruct((2 * local + 1, tile, tile), jnp.bfloat16),
        ],
        in_specs=[SMEM, VMEM, VMEM, VMEM, VMEM],
        out_specs=[VMEM, VMEM],
        scratch_shapes=[pltpu.VMEM((aux, width), jnp.float32)],
        compiler_params=params(16),
        name="intermediate",
    )(in_smem(table), own, other, rows, start)


def step(table, next_orbs, mine, arrival, *, plain):
    length = arrival.shape[0] - LABEL

    def body(table, next_orbs, mine, arrival, kept, out):
        value = mine[:length, :].astype(jnp.float32)
        extra = arrival[:length, :].astype(jnp.float32)
        own = jnp.zeros((LABEL, LANES), jnp.float32) + table[FACTS, ORBITAL].astype(jnp.float32)
        out[length:, :] = own.astype(out.dtype)

        @pl.when(table[FACTS, CORE] == plain)
        def _():
            total = value + extra
            kept[...] = total
            out[:length, :] = total.astype(out.dtype)

        @pl.when(table[FACTS, CORE] != plain)
        def _():
            label = own[:1, :]
            theirs = arrival[length : length + LABEL, :].astype(jnp.float32)[:1, :]
            behind = next_orbs[0:1, 1:2].astype(jnp.float32)
            kept[...] = value + jnp.where(theirs == label, extra, 0.0)
            out[:length, :] = (
                jnp.where(label == behind, value, 0.0) + jnp.where(theirs == behind, extra, 0.0)
            ).astype(out.dtype)

    return pl.pallas_call(
        body,
        out_shape=[
            jax.ShapeDtypeStruct((length, LANES), jnp.float32),
            jax.ShapeDtypeStruct(arrival.shape, arrival.dtype),
        ],
        in_specs=[SMEM, VMEM, VMEM, VMEM],
        out_specs=[VMEM, VMEM],
        compiler_params=params(16),
        name="step",
    )(in_smem(table), next_orbs, mine, arrival)


def last_step(mine, arrival):
    length = mine.shape[0]

    def body(mine, arrival, out):
        out[...] = (mine[...] + arrival[:length, :].astype(jnp.float32)).astype(out.dtype)

    return pl.pallas_call(
        body,
        out_shape=jax.ShapeDtypeStruct(mine.shape, arrival.dtype),
        in_specs=[VMEM, VMEM],
        out_specs=VMEM,
        compiler_params=params(16),
        name="last_step",
    )(mine, arrival)


def ladder_build(table, held, factor):
    empty, tile = held.shape[0] - 1, held.shape[1]
    width = factor.shape[0]
    tiles = width // tile
    pairs = -(-tiles // 2)

    def body(table, held, source, left, factor, wide, state, sems):
        def load(c):
            here = block(c, tile)
            return pltpu.make_async_copy(source.at[:, here], factor.at[:, here], sems.at[c])

        def start(c):
            @pl.when(state[c] == 0)
            def _():
                load(c).start()
                state[c] = 1

        def wait(c):
            @pl.when(state[c] == 1)
            def _():
                load(c).wait()
                state[c] = 2

        for c in range(tiles):
            state[c] = 0
        used = table[FACTS, USED]
        kept = table[BEGIN, used]

        def start_slot(k, carry):
            start(table[COLUMN, table[SORTED, k]])
            return carry

        def start_rest(c, carry):
            start(c)
            return carry

        lax.fori_loop(0, kept, start_slot, 0)
        lax.fori_loop(0, tiles, start_rest, 0)

        def two_tiles(m, carry):
            first, second, end = [table[BEGIN, 2 * m + k] for k in range(3)]
            here = block(m, 2 * tile)

            def wait_slot(k, carry):
                wait(table[COLUMN, table[SORTED, k]])
                return carry

            lax.fori_loop(first, end, wait_slot, 0)

            def product(at, count):
                columns, weights = [], []
                for k in range(count):
                    there = at + k < end
                    s = table[SORTED, jnp.where(there, at + k, first)]
                    columns.append(factor[:, block(table[COLUMN, s], tile)])
                    value, none = held[jnp.where(there, s, empty)], jnp.zeros((tile, tile), held.dtype)
                    early = at + k < second
                    weights.append(
                        jnp.concatenate([jnp.where(early, value, none), jnp.where(early, none, value)], axis=1)
                    )
                return jnp.dot(
                    jnp.concatenate(columns, axis=1), jnp.concatenate(weights, axis=0),
                    preferred_element_type=jnp.float32,
                )

            rounds = (end - first + 1) // 2
            for n in range(1, 4):

                @pl.when(rounds == n)
                def _():
                    left[:, here] = product(first, 2 * n).astype(left.dtype)

            @pl.when(rounds > 3)
            def _():
                wide[...] = product(first, 2)

                def add(t, carry):
                    wide[...] += product(first + 2 * t, 2)
                    return carry

                lax.fori_loop(1, rounds, add, 0)
                left[:, here] = wide[...].astype(left.dtype)

            return carry

        lax.fori_loop(0, (used + 1) // 2, two_tiles, 0)

        def wait_rest(c, carry):
            wait(c)
            return carry

        lax.fori_loop(0, tiles, wait_rest, 0)

    return pl.pallas_call(
        body,
        out_shape=[
            jax.ShapeDtypeStruct((width, 2 * pairs * tile), jnp.bfloat16),
            jax.ShapeDtypeStruct(factor.shape, factor.dtype),
        ],
        in_specs=[SMEM, VMEM, HBM],
        out_specs=[VMEM, VMEM],
        scratch_shapes=[
            pltpu.VMEM((width, 2 * tile), jnp.float32),
            pltpu.SMEM((tiles,), jnp.int32),
            pltpu.SemaphoreType.DMA((tiles,)),
        ],
        compiler_params=params(32),
        cost_estimate=pl.CostEstimate(flops=10**10, bytes_accessed=1, transcendentals=0),
        name="ladder_build",
    )(in_smem(table), held, in_hbm(factor))


def ladder_multiply(table, left, factor, tile, *, far, flops):
    half = left.shape[0] // 2

    def body(table, left, factor, out):
        core = table[FACTS, CORE]
        rows = block(1 - core if far else core, half)
        steps = (table[FACTS, USED] + 1) // 2
        for n in range(factor.shape[0] // tile // 2 + 1):

            @pl.when(steps == n)
            def _():
                def unit(k, carry):
                    if n == 0:
                        out[k] = jnp.zeros((half, half), out.dtype)
                        return carry
                    here = block(k, half)
                    right = jnp.concatenate(
                        [factor[here, block(table[NAME, w], tile)] for w in range(2 * n)], axis=1
                    )
                    out[k] = lax.dot_general(
                        left[rows, : 2 * n * tile], right, LAST_LAST, preferred_element_type=jnp.float32
                    ).astype(out.dtype)
                    return carry

                lax.fori_loop(0, 2, unit, 0, unroll=True)

    return ladder_call(body, (2, half, half), [], in_smem(table), left, factor, flops=flops)


def ladder_call(body, shape, scratch, *operands, flops):
    return pl.pallas_call(
        body,
        out_shape=jax.ShapeDtypeStruct(shape, jnp.bfloat16),
        in_specs=[SMEM] + [VMEM] * (len(operands) - 1),
        out_specs=VMEM,
        scratch_shapes=scratch,
        compiler_params=params(32),
        cost_estimate=pl.CostEstimate(flops=flops, bytes_accessed=1, transcendentals=0),
        name="ladder",
    )(*operands)


def finish(table, sums, near, arrived, cycle_rows, whole, *, pieces):
    half = arrived.shape[1]
    aux = cycle_rows.shape[1]
    rows = half // pieces
    first = whole is None

    def body(table, sums, near, arrived, factor, *refs):
        out, low, done, sems = refs[-4:]
        core = table[FACTS, CORE]
        side = core if first else 1 - core
        for n in range(half // LANES):
            low[:, n * LANES : (n + 1) * LANES] = sums[n * aux : (n + 1) * aux, :]
        stores = []
        for n in range(pieces):
            here = slice(n * rows, (n + 1) * rows)
            term = jnp.dot(
                factor[pl.ds(pl.multiple_of(core * half + n * rows, rows), rows), :], low[...],
                preferred_element_type=jnp.float32,
            )
            ladder = near[side, here, :].astype(jnp.float32) + arrived[side, here, :].astype(jnp.float32)
            total = ladder + term
            done[here, :] = total.astype(done.dtype)
            store = pltpu.make_async_copy(
                done.at[here, :], out.at[here, block(side, half)], sems.at[n]
            )
            store.start()
            stores.append(store)
        for store in stores:
            store.wait()

    operands = [in_smem(table), sums, near, arrived, cycle_rows]
    return pl.pallas_call(
        body,
        out_shape=jax.ShapeDtypeStruct((half, 2 * half), jnp.bfloat16),
        in_specs=[SMEM] + [VMEM] * 4 + [HBM] * (not first),
        out_specs=HBM,
        scratch_shapes=[
            pltpu.VMEM((aux, half), jnp.bfloat16),
            pltpu.VMEM((half, half), jnp.bfloat16),
            pltpu.SemaphoreType.DMA((pieces,)),
        ],
        input_output_aliases={} if first else {len(operands): 0},
        compiler_params=params(16),
        cost_estimate=pl.CostEstimate(flops=10**9, bytes_accessed=1, transcendentals=0),
        name="finish_own" if first else "finish_other",
    )(*operands, *([] if first else [whole]))


def shards(amp_tiles, tile_coords, tile_mask, pair_orbs, ladder_factor, cycle_factor):
    cores, pairs = lax.axis_size("virt"), lax.axis_size("pair")
    assert cores == 2 and pairs % 2 == 0
    own = amp_tiles[0]
    place = lax.axis_index("virt").astype(jnp.int32).reshape(1)
    swap = [(0, 1), (1, 0)]
    other = lax.ppermute(own, "virt", swap)
    square = pairs == 8
    table, own, cycle_rows, start = prepare(tile_coords[0].T, tile_mask, pair_orbs, place, own, cycle_factor, cores=cores)
    message, held = intermediate(table, own, other, cycle_rows, start)
    factor = ladder_factor[0]
    tile = held.shape[1]

    def exchange(value, *partners):
        routes = [(p * 2 + c, (p ^ partners[c]) * 2 + c) for p in range(pairs) for c in range(2)]
        return lax.ppermute(value, ("pair", "virt"), routes)

    if square:
        arrival = exchange(message, ORDERS[0][0], ORDERS[1][0])
        message, pair_orbs, held, factor = lax.optimization_barrier((message, pair_orbs, held, factor))
        next_orbs = exchange(pair_orbs, ORDERS[0][2], ORDERS[1][1])
        left, factor = ladder_build(table, held, factor)
        arrival, left = lax.optimization_barrier((arrival, left))
        kept, message = step(table, next_orbs, message, arrival, plain=0)
        message, left = lax.optimization_barrier((message, left))
        arrival = exchange(message, ORDERS[0][1], ORDERS[1][1])
        far = ladder_multiply(table, left, factor, tile, far=True, flops=10**10)
        arrival, far = lax.optimization_barrier((arrival, far))
        kept, message = step(table, next_orbs, kept, arrival, plain=1)
        message, left, far = lax.optimization_barrier((message, left, far))
        arrival = exchange(message, ORDERS[0][2], ORDERS[1][2])
        arrived = lax.ppermute(far, "virt", swap)
        near = ladder_multiply(table, left, factor, tile, far=False, flops=4 * 10**10)
        arrival, near = lax.optimization_barrier((arrival, near))
        sums = last_step(kept, arrival)
    else:
        left, factor = ladder_build(table, held, factor)
        far = ladder_multiply(table, left, factor, tile, far=True, flops=10**10)
        near = ladder_multiply(table, left, factor, tile, far=False, flops=10**10)
        arrived = lax.ppermute(far, "virt", swap)
        right = pair_orbs[0, 1]
        occupied = jnp.arange(cycle_factor.shape[0], dtype=jnp.int32) == right
        mine = message[:-LABEL].astype(jnp.float32)
        total = lax.psum(jnp.where(occupied[:, None, None], mine[None], 0.0), "pair")
        sums = lax.dynamic_index_in_dim(total, right, 0, keepdims=False).astype(jnp.bfloat16)

    other_sums = lax.ppermute(sums, "virt", swap)
    own_side = finish(table, sums, near, arrived, cycle_rows, None, pieces=4)
    return finish(table, other_sums, near, arrived, cycle_rows, own_side, pieces=4)[None]


def solution(mesh):
    in_specs = (
        P(("groups", "pair"), "virt", None, None),
        P(("groups", "pair"), None, None),
        P(("groups", "pair"), None),
        P(("groups", "pair"), None),
        P(("groups", "virt"), None, None),
        P("groups", None, None),
    )
    out_specs = P(("groups", "pair"), "virt", None)
    return jax.shard_map(shards, mesh=mesh, in_specs=in_specs, out_specs=out_specs, check_vma=False)
```
